512 devices in a mesh: dp: 64 (over z_lo, x, core), tensor: 8 (over z_hi, y).
Axes of the slice: x: 4, y: 4, z: 16 (z_hi: 2, z_lo: 8; z = z_hi * 8 + z_lo), core: 2. Of those that a mesh axis runs over, the one named last changes fastest.
Arguments:
- visits: bfloat16 [8192, 4096], P('dp'), may hold values from -6 to 6
- notes: bfloat16 [8192, 4096], P('dp'), may hold values from -6 to 6
- visit_weight: bfloat16 [4096, 1024], P('dp', 'tensor'), may hold values from -0.09375 to 0.09375
- note_weight: bfloat16 [4096, 1024], P('dp', 'tensor'), may hold values from -0.09375 to 0.09375
- patient_ids: int32 [8192], replicated, may hold values from 0 to 4095
- loss_grad: float32 [1], replicated, may hold values from 64 to 256
Outputs:
- visit_weight_grad: float32 [4096, 1024], P('dp', 'tensor')
- note_weight_grad: float32 [4096, 1024], P('dp', 'tensor')
The draws below stay inside these ranges and needn't reach their ends.
Inputs may be any that keep to these rules, and one draw needn't show every extreme that they name: `patient_ids`: pairs with equal ids are positive pairs; every pair is positive with itself.
All inputs are finite; a program needn't handle non-finite values.
Results may differ from the reference program's by a relative error of at most 0.015.
Values may be sent and summed in bfloat16 or wider, within the bound.
A program may use at most 64 MiB of HBM per device.

```python
import math
import jax
import jax.numpy as jnp
from jax import lax

H = 4096
E = 1024
TOK_DEV = 128
TOKENS = 8192
N_DP = 64
N_TENSOR = 8


def with_ends(array, stream_key, low, top_value):
    longest = array.shape.index(max(array.shape))
    spots = []
    for shift in (0, 1):
        where = [jax.random.randint(jax.random.fold_in(stream_key, axis), (), 0, length) for axis, length in enumerate(array.shape)]
        where[longest] = (where[longest] + shift) % array.shape[longest]
        spots.append(tuple(where))
    return array.at[spots[0]].set(low).at[spots[1]].set(top_value)


def block_scale(key, extent, split, least, largest):
    factor_of, own = 1.0, jax.random.fold_in(key, 6)
    for axis_at, parts in split:
        draws = jnp.exp(jax.random.uniform(jax.random.fold_in(own, axis_at), (parts,), jnp.float32, least / len(split), largest / len(split)))
        factor_of = factor_of * jnp.repeat(draws, extent[axis_at] // parts).reshape([-1 if axis == axis_at else 1 for axis in range(len(extent))])
    return factor_of


def noise(stream_key, extent, spread, most, cuts=(), held_as=jnp.bfloat16):
    gain = block_scale(stream_key, extent, cuts, -0.22, 0.18) if cuts else 1.0
    values = jax.random.normal(stream_key, extent, jnp.float32) * spread * gain
    return jnp.minimum(jnp.maximum(values, -most), most).astype(held_as)


def setup_inputs(seed: int = 0) -> dict:
    splits = jax.random.split(jax.random.key(seed), 7)
    visits = noise(splits[0], (TOKENS, H), 1.0, 6.0, ((0, 64),))
    notes = noise(splits[1], (TOKENS, H), 1.0, 6.0, ((0, 64),))
    visit_weight = noise(splits[2], (H, E), H ** -0.5, 0.09375, ((0, 64), (1, 8)))
    note_weight = noise(splits[3], (H, E), H ** -0.5, 0.09375, ((0, 64), (1, 8)))
    patient_ids = with_ends(jax.random.randint(splits[4], (TOKENS,), 0, TOKENS // 2), jax.random.fold_in(splits[4], 1), 0, (TOKENS // 2) - 1).astype(jnp.int32)
    loss_grad = jnp.clip(jnp.exp(jax.random.uniform(splits[5], (1,), jnp.float32, math.log(64.0), math.log(256.0))), 64.0, 256.0)
    return {"visits": visits, "notes": notes, "visit_weight": visit_weight, "note_weight": note_weight, "patient_ids": patient_ids, "loss_grad": loss_grad}


SCALE = 10.0
BIAS = -2.0
EPS = 1e-06

def reference(visits, notes, visit_weight, note_weight, patient_ids, loss_grad):
    proj_visit = jnp.dot(visits, visit_weight, preferred_element_type=jnp.float32)
    proj_note = jnp.dot(notes, note_weight, preferred_element_type=jnp.float32)
    norm_visit = jnp.sqrt(lax.optimization_barrier(jnp.sum(proj_visit * proj_visit, axis=1, keepdims=True)) + EPS)
    norm_note = jnp.sqrt(lax.optimization_barrier(jnp.sum(proj_note * proj_note, axis=1, keepdims=True)) + EPS)
    unit_visit = proj_visit / norm_visit
    unit_note = proj_note / norm_note
    visit_low = unit_visit.astype(jnp.bfloat16)
    note_low = unit_note.astype(jnp.bfloat16)
    width = E // N_TENSOR
    factor = SCALE * loss_grad[0] / TOKENS

    def block(d_note, start):
        rows = lax.dynamic_slice_in_dim(visit_low, start, TOK_DEV, 0)
        own_ids = lax.dynamic_slice_in_dim(patient_ids, start, TOK_DEV, 0)
        summed = jnp.zeros((TOK_DEV, TOKENS), jnp.float32)
        for group in range(N_TENSOR):
            part = jnp.dot(rows[:, group * width:(group + 1) * width], note_low[:, group * width:(group + 1) * width].T, preferred_element_type=jnp.float32).astype(jnp.bfloat16)
            part = lax.optimization_barrier(part)
            summed = summed + part.astype(jnp.float32)
        logit = SCALE * summed + BIAS
        sign = jnp.where(own_ids[:, None] == patient_ids[None, :], 1.0, -1.0).astype(jnp.float32)
        weights = (factor * -sign * jax.nn.sigmoid(-sign * logit)).astype(jnp.bfloat16)
        d_rows = jnp.dot(weights, note_low, preferred_element_type=jnp.float32)
        d_note = d_note + jnp.dot(weights.T, rows, preferred_element_type=jnp.float32)
        return (d_note, d_rows)
    starts = jnp.arange(N_DP, dtype=jnp.int32) * TOK_DEV
    d_note, d_blocks = lax.scan(block, jnp.zeros((TOKENS, E), jnp.float32), starts)
    d_visit = d_blocks.reshape(TOKENS, E)
    dot_visit = lax.optimization_barrier(jnp.sum(unit_visit * d_visit, axis=1, keepdims=True))
    dot_note = lax.optimization_barrier(jnp.sum(unit_note * d_note, axis=1, keepdims=True))
    grad_visit = ((d_visit - unit_visit * dot_visit) / norm_visit).astype(jnp.bfloat16)
    grad_note = ((d_note - unit_note * dot_note) / norm_note).astype(jnp.bfloat16)
    visit_weight_grad = jnp.dot(visits.T, grad_visit, preferred_element_type=jnp.float32)
    note_weight_grad = jnp.dot(notes.T, grad_note, preferred_element_type=jnp.float32)
    return (visit_weight_grad, note_weight_grad)
```

```python
import functools

import jax
import jax.numpy as jnp
from jax import lax
from jax.experimental import pallas as pl
from jax.experimental.pallas import tpu as pltpu
from jax.sharding import PartitionSpec as P

SCALE = 10.0
BIAS = -2.0
EPS = 1e-06
F32 = jnp.float32
LOW = jnp.bfloat16
NT = (((1,), (1,)), ((), ()))
TN = (((0,), (0,)), ((), ()))
NX, NY = 4, 4


def flip(value, bit):
    return 1 - value if bit else value


def kernel(
    total,
    visits, notes, visit_weight, note_weight, own_ids, pair_ids, loss_grad,
    visit_out, note_out,
    heads, projs, proj_own, inverse, units, pairs,
    d_own, d_send, d_recv, d_last_send, d_last_recv, dots,
    own_part, core_send, core_recv, x_send, x_recv, z_own, z_send, z_recv,
    head_sent, head_got, proj_sent, proj_got, pair_sent, pair_got,
    d_sent, d_got, grad_sent, grad_got,
):
    dp, tensor = lax.axis_index("dp"), lax.axis_index("tensor")
    c, x, z = lax.rem(dp, 2), lax.rem(lax.div(dp, 2), NX), lax.div(dp, 2 * NX)
    h, q1, q2 = lax.rem(z, 2), lax.rem(lax.div(z, 2), 2), lax.div(z, 4)
    q = lax.div(z, 2)
    y, half = lax.rem(tensor, NY), lax.div(tensor, NY)

    def pair_of(g):
        return flip(q2, g // 2) * 2 + flip(q1, g % 2)

    def at(zz, xx, cc):
        return ((zz * NX + xx) * 2 + cc, tensor)

    def z_peer(k):
        return at(pair_of(k // 2) * 2 + flip(h, k % 2), x, c)

    def x_right(k):
        return lax.rem(x + k, NX)

    def x_left(k):
        return lax.rem(x + NX - k, NX)

    def x_peer(k):
        return at(z, x_right(k), c)

    def y_right(k):
        return lax.rem(y + k, NY)

    def y_left(k):
        return lax.rem(y + NY - k, NY)

    def y_peer(k):
        return (dp, half * NY + y_right(k))

    core_peer = at(z, x, 1 - c)
    half_peer = (dp, (1 - half) * NY + y)

    started = []

    def send(src, dst, sent, got, peer):
        copy = pltpu.make_async_remote_copy(
            src_ref=src, dst_ref=dst, send_sem=sent, recv_sem=got,
            device_id=peer, device_id_type=pl.DeviceIdType.MESH,
        )
        copy.start()
        started.append(copy)

    def arrived(dst, sent, got, peer):
        pltpu.make_async_remote_copy(
            src_ref=dst, dst_ref=dst, send_sem=sent, recv_sem=got,
            device_id=peer, device_id_type=pl.DeviceIdType.MESH,
        ).wait_recv()

    peers = (
        [z_peer(k) for k in range(1, 8)] + [x_peer(k) for k in range(1, 4)]
        + [y_peer(k) for k in range(1, 4)] + [core_peer, half_peer]
    )
    barrier = pltpu.get_barrier_semaphore()
    for peer in peers:
        pl.semaphore_signal(barrier, inc=1, device_id=peer, device_id_type=pl.DeviceIdType.MESH)

    def gather_start(buf, sent, got):
        mine = buf.at[:, q, h, x, c]
        for k in range(1, 8):
            send(mine, mine, sent.at[k], got.at[k], z_peer(k))

    def gather_rest(buf, sent, got):
        for g in range(4):
            for b in range(2):
                k = 2 * g + b
                if k:
                    arrived(buf.at[:, pair_of(g), flip(h, b), x, c], sent.at[k], got.at[k], z_peer(k))
            block = buf.at[:, pair_of(g), :, x, c]
            for k in (2, 1, 3):
                n = 8 + k * 4 + g
                send(block, block, sent.at[n], got.at[n], x_peer(k))
            send(block, block, sent.at[24 + g], got.at[24 + g], core_peer)
        for g in range(4):
            for k in (1, 3, 2):
                block = buf.at[:, pair_of(g), :, x_left(k), c]
                n = 8 + k * 4 + g
                arrived(block, sent.at[n], got.at[n], x_peer(k))
                m = 24 + k * 4 + g
                send(block, block, sent.at[m], got.at[m], core_peer)
        for g in range(4):
            for k in range(4):
                m = 24 + k * 4 + g
                arrived(
                    buf.at[:, pair_of(g), :, x_left(k), 1 - c], sent.at[m], got.at[m], core_peer
                )

    heads[0, q, h, x, c] = visit_weight[...]
    heads[1, q, h, x, c] = note_weight[...]
    pl.semaphore_wait(barrier, len(peers))
    gather_start(heads, head_sent, head_got)
    gather_rest(heads, head_sent, head_got)

    for a, rows in ((0, visits), (1, notes)):
        head = heads[a].reshape(rows.shape[1], 128)
        proj = jnp.dot(rows[...], head, preferred_element_type=F32)
        proj_own[a] = proj
        projs[a, half, y] = proj.astype(LOW)
    mine = projs.at[:, half, y]
    other = projs.at[:, 1 - half, y]
    send(mine, mine, proj_sent.at[0], proj_got.at[0], half_peer)
    for k in (2, 1, 3):
        send(mine, mine, proj_sent.at[k], proj_got.at[k], y_peer(k))
    arrived(other, proj_sent.at[0], proj_got.at[0], half_peer)
    for k in (2, 1, 3):
        send(other, other, proj_sent.at[4 + k], proj_got.at[4 + k], y_peer(k))
    for k in range(1, 4):
        arrived(projs.at[:, half, y_left(k)], proj_sent.at[k], proj_got.at[k], y_peer(k))
    for k in range(1, 4):
        arrived(projs.at[:, 1 - half, y_left(k)], proj_sent.at[4 + k], proj_got.at[4 + k], y_peer(k))

    def normalised(a, rows):
        parts = [projs[a, t // NY, t % NY, rows, :].astype(F32) for t in range(8)]
        squares = parts[0] * parts[0]
        for part in parts[1:]:
            squares = squares + part * part
        scale = lax.rsqrt(jnp.sum(squares, axis=1, keepdims=True) + EPS)
        return scale, [(part * scale).astype(LOW) for part in parts]

    for a in range(2):
        _, low = normalised(a, pl.ds(pl.multiple_of(tensor * 16, 16), 16))
        for t in range(8):
            pairs[a, q, h, x, c, :, t * 128:(t + 1) * 128] = low[t]
    gather_start(pairs, pair_sent, pair_got)
    for a in range(2):
        scale, low = normalised(a, slice(None))
        inverse[a] = jnp.broadcast_to(scale, (128, 128))
        for t in range(8):
            units[a, :, t * 128:(t + 1) * 128] = low[t]
    gather_rest(pairs, pair_sent, pair_got)

    factor = SCALE * loss_grad[0] / total
    minus_sign = jnp.where(own_ids[...] == pair_ids[...], -1.0, 1.0).astype(F32)
    sums = []
    for a in range(2):
        others = pairs[1 - a].reshape(1024, 1024)
        summed = lax.dot_general(units[a], others, NT, preferred_element_type=F32)
        logit = SCALE * summed + BIAS
        weights = (factor * minus_sign * jax.nn.sigmoid(minus_sign * logit)).astype(LOW)
        sums.append(jnp.sum(weights.astype(F32) * summed, axis=1, keepdims=True))
        d = jnp.dot(weights, others, preferred_element_type=F32)
        for t in range(8):
            piece = d[:, t * 128:(t + 1) * 128]
            d_own[t // NY, t % NY, a] = piece
            d_send[t // NY, t % NY, a] = piece.astype(LOW)
    lane = lax.broadcasted_iota(jnp.int32, (128, 128), 1)
    dots[0] = jnp.transpose(jnp.where(lane == 0, sums[0], sums[1]))[:8]

    for k in (2, 1, 3):
        send(d_send.at[1 - half, y_right(k)], d_recv.at[0, k], d_sent.at[k], d_got.at[k], y_peer(k))
        send(dots.at[0], dots.at[k], d_sent.at[4 + k], d_got.at[4 + k], y_peer(k))
    for k in (2, 1, 3):
        send(d_send.at[half, y_right(k)], d_recv.at[1, k], d_sent.at[8 + k], d_got.at[8 + k], y_peer(k))
    for k in range(1, 4):
        arrived(d_recv.at[0, k], d_sent.at[k], d_got.at[k], y_peer(k))
        arrived(dots.at[k], d_sent.at[4 + k], d_got.at[4 + k], y_peer(k))
    away = d_own[1 - half, y]
    for k in range(1, 4):
        away = away + d_recv[0, k].astype(F32)
    d_last_send[...] = away.astype(LOW)
    send(d_last_send, d_last_recv, d_sent.at[0], d_got.at[0], half_peer)
    dots[4] = dots[0] + dots[1] + dots[2] + dots[3]
    send(dots.at[4], dots.at[5], d_sent.at[4], d_got.at[4], half_peer)
    for k in range(1, 4):
        arrived(d_recv.at[1, k], d_sent.at[8 + k], d_got.at[8 + k], y_peer(k))
    d = d_own[half, y]
    for k in range(1, 4):
        d = d + d_recv[1, k].astype(F32)
    arrived(d_last_recv, d_sent.at[0], d_got.at[0], half_peer)
    arrived(dots.at[5], d_sent.at[4], d_got.at[4], half_peer)
    d = d + d_last_recv[...].astype(F32)
    dot_rows = dots[4] + dots[5]
    grads = []
    for a in range(2):
        dot = jnp.transpose(jnp.broadcast_to(dot_rows[a:a + 1], (128, 128)))
        scale = inverse[a]
        grads.append(((d[a] - proj_own[a] * scale * dot) * scale).astype(LOW))

    for k in (2, 1, 3, 0):
        for a, rows in ((0, visits), (1, notes)):
            for zz in range(8):
                columns = pl.ds(pl.multiple_of((zz * NX + x_right(k)) * 128, 128), 128)
                part = lax.dot_general(rows[:, columns], grads[a], TN, preferred_element_type=F32)
                part = part.reshape(2, 64, 128)
                first, second = part[0], part[1]
                own_part[k, a, zz // 2, zz % 2] = jnp.where(c == 0, first, second)
                core_send[k, a, zz // 2, zz % 2] = jnp.where(c == 0, second, first).astype(LOW)
        send(core_send.at[k], core_recv.at[k], grad_sent.at[k], grad_got.at[k], core_peer)
    for k in (2, 1, 3):
        arrived(core_recv.at[k], grad_sent.at[k], grad_got.at[k], core_peer)
        x_send[k] = (own_part[k] + core_recv[k].astype(F32)).astype(LOW)
        send(x_send.at[k], x_recv.at[k], grad_sent.at[4 + k], grad_got.at[4 + k], x_peer(k))
    arrived(core_recv.at[0], grad_sent.at[0], grad_got.at[0], core_peer)
    z_own[...] = own_part[0] + core_recv[0].astype(F32)
    for k in (1, 3, 2):
        arrived(x_recv.at[k], grad_sent.at[4 + k], grad_got.at[4 + k], x_peer(k))
        z_own[...] += x_recv[k].astype(F32)
    z_send[...] = z_own[...].astype(LOW)
    for k in range(1, 8):
        send(
            z_send.at[:, pair_of(k // 2), flip(h, k % 2)], z_recv.at[k],
            grad_sent.at[8 + k], grad_got.at[8 + k], z_peer(k),
        )
    done = z_own[:, q, h]
    for k in range(1, 8):
        arrived(z_recv.at[k], grad_sent.at[8 + k], grad_got.at[8 + k], z_peer(k))
        done = done + z_recv[k].astype(F32)
    visit_out[...] = done[0]
    note_out[...] = done[1]
    for copy in started:
        copy.wait_send()


def local(visits, notes, visit_weight, note_weight, patient_ids, loss_grad):
    rows = visits.shape[0]
    total = patient_ids.shape[0]
    dp, tensor = lax.axis_index("dp"), lax.axis_index("tensor")
    own_ids = lax.dynamic_slice_in_dim(patient_ids, dp * rows, rows, 0).reshape(rows, 1)
    pair_ids = lax.dynamic_slice_in_dim(
        patient_ids.reshape(total // rows, rows), tensor * 16, 16, 1
    ).reshape(1, -1)
    vmem = pl.BlockSpec(memory_space=pltpu.VMEM)
    grad = jax.ShapeDtypeStruct(visit_weight.shape, F32)
    sems = pltpu.SemaphoreType.DMA
    return pl.pallas_call(
        functools.partial(kernel, total),
        out_shape=(grad, grad),
        in_specs=[vmem] * 6 + [pl.BlockSpec(memory_space=pltpu.SMEM)],
        out_specs=(vmem, vmem),
        scratch_shapes=[
            pltpu.VMEM((2, 4, 2, 4, 2, 64, 128), LOW),
            pltpu.VMEM((2, 2, 4, 128, 128), LOW),
            pltpu.VMEM((2, 128, 128), F32),
            pltpu.VMEM((2, 128, 128), F32),
            pltpu.VMEM((2, 128, 1024), LOW),
            pltpu.VMEM((2, 4, 2, 4, 2, 16, 1024), LOW),
            pltpu.VMEM((2, 4, 2, 128, 128), F32),
            pltpu.VMEM((2, 4, 2, 128, 128), LOW),
            pltpu.VMEM((2, 4, 2, 128, 128), LOW),
            pltpu.VMEM((2, 128, 128), LOW),
            pltpu.VMEM((2, 128, 128), LOW),
            pltpu.VMEM((6, 8, 128), F32),
            pltpu.VMEM((4, 2, 4, 2, 64, 128), F32),
            pltpu.VMEM((4, 2, 4, 2, 64, 128), LOW),
            pltpu.VMEM((4, 2, 4, 2, 64, 128), LOW),
            pltpu.VMEM((4, 2, 4, 2, 64, 128), LOW),
            pltpu.VMEM((4, 2, 4, 2, 64, 128), LOW),
            pltpu.VMEM((2, 4, 2, 64, 128), F32),
            pltpu.VMEM((2, 4, 2, 64, 128), LOW),
            pltpu.VMEM((8, 2, 64, 128), LOW),
            sems((40,)), sems((40,)),
            sems((8,)), sems((8,)),
            sems((40,)), sems((40,)),
            sems((12,)), sems((12,)),
            sems((16,)), sems((16,)),
        ],
        compiler_params=pltpu.CompilerParams(
            collective_id=0, has_side_effects=True, vmem_limit_bytes=48 * 1024 * 1024
        ),
    )(visits, notes, visit_weight, note_weight, own_ids, pair_ids, loss_grad)


def solution(mesh):
    return jax.shard_map(
        local,
        mesh=mesh,
        in_specs=(P("dp", None), P("dp", None), P("dp", "tensor"), P("dp", "tensor"), P(), P()),
        out_specs=(P("dp", "tensor"), P("dp", "tensor")),
        check_vma=False,
    )
```

```python
import functools

import jax
import jax.numpy as jnp
from jax import lax
from jax.experimental import pallas as pl
from jax.experimental.pallas import tpu as pltpu
from jax.sharding import PartitionSpec as P

SCALE = 10.0
BIAS = -2.0
EPS = 1e-06
F32 = jnp.float32
LOW = jnp.bfloat16
NT = (((1,), (1,)), ((), ()))
TN = (((0,), (0,)), ((), ()))
NX, NY = 4, 4


def flip(value, bit):
    return 1 - value if bit else value


def kernel(
    total,
    visits_in, notes_in, visit_weight, note_weight, own_ids, pair_ids, loss_grad,
    visit_out, note_out,
    features, heads, projs, proj_own, inverse, units, pairs,
    d_own, d_send, d_recv, d_last, dots,
    own_part, core_send, core_recv, x_send, x_recv, z_own, z_send, z_recv,
    load_done, head_sent, head_got, proj_sent, proj_got, pair_sent, pair_got,
    d_sent, d_got, grad_sent, grad_got,
):
    dp, tensor = lax.axis_index("dp"), lax.axis_index("tensor")
    c, x, z = lax.rem(dp, 2), lax.rem(lax.div(dp, 2), NX), lax.div(dp, 2 * NX)
    z0, z1, z2 = lax.rem(z, 2), lax.rem(lax.div(z, 2), 2), lax.div(z, 4)
    y, half = lax.rem(tensor, NY), lax.div(tensor, NY)
    left, right = lax.rem(x + NX - 1, NX), lax.rem(x + 1, NX)
    beyond = lax.rem(x + 2, NX)

    def low(j):
        return flip(z1, j // 2) * 2 + flip(z0, j % 2)

    def high(f):
        return flip(z2, f)

    def at(zz, xx, cc):
        return ((zz * NX + xx) * 2 + cc, tensor)

    def z_peer(k):
        return at(high(k // 4) * 4 + low(k % 4), x, c)

    def x_right(k):
        return lax.rem(x + k, NX)

    def x_peer(k):
        return at(z, x_right(k), c)

    def y_right(k):
        return lax.rem(y + k, NY)

    def y_left(k):
        return lax.rem(y + NY - k, NY)

    def y_peer(k):
        return (dp, half * NY + y_right(k))

    core_peer = at(z, x, 1 - c)
    half_peer = (dp, (1 - half) * NY + y)
    middle_peer = (((1 - z2) * 4 + low(0)) * NX * 2 + x * 2 + c, (1 - half) * NY + y)

    started = []

    def send(src, dst, sent, got, n, peer):
        copy = pltpu.make_async_remote_copy(
            src_ref=src, dst_ref=dst, send_sem=sent.at[n], recv_sem=got.at[n],
            device_id=peer, device_id_type=pl.DeviceIdType.MESH,
        )
        copy.start()
        started.append(copy)

    def arrived(dst, sent, got, n, peer):
        pltpu.make_async_remote_copy(
            src_ref=dst, dst_ref=dst, send_sem=sent.at[n], recv_sem=got.at[n],
            device_id=peer, device_id_type=pl.DeviceIdType.MESH,
        ).wait_recv()

    peers = (
        [z_peer(k) for k in range(1, 5)] + [x_peer(k) for k in range(1, 4)]
        + [y_peer(k) for k in range(1, 4)] + [core_peer, middle_peer]
    )
    barrier = pltpu.get_barrier_semaphore()
    for peer in peers:
        pl.semaphore_signal(barrier, inc=1, device_id=peer, device_id_type=pl.DeviceIdType.MESH)

    def gather(buf, sent, got):
        def block(j, f, xx):
            return buf.at[high(f), low(j), xx, c]

        def to_x(j, f):
            here = block(j, f, x)
            send(here, here, sent, got, 8 + 2 * j + f, x_peer(1))
            send(here, here, sent, got, 16 + 2 * j + f, x_peer(3))

        def to_core(j, n, xx):
            chunk = buf.at[:, low(j), xx, c]
            send(chunk, chunk, sent, got, 32 + 4 * n + j, core_peer)

        mine = block(0, 0, x)
        send(mine, mine, sent, got, 0, z_peer(4))
        for j in (3, 2, 1):
            send(mine, mine, sent, got, j, z_peer(j))
        to_x(0, 0)
        yield
        for j in (1, 2, 3):
            arrived(block(j, 0, x), sent, got, j, z_peer(j))
            to_x(j, 0)
        yield
        far = block(0, 1, x)
        arrived(far, sent, got, 0, z_peer(4))
        for j in (3, 2, 1):
            send(far, far, sent, got, 4 + j, z_peer(j))
        to_x(0, 1)
        to_core(0, 0, x)
        yield
        for j in range(4):
            theirs = block(j, 0, left)
            arrived(theirs, sent, got, 8 + 2 * j, x_peer(3))
            send(theirs, theirs, sent, got, 24 + 2 * j, x_peer(1))
            arrived(block(j, 0, right), sent, got, 16 + 2 * j, x_peer(1))
        yield
        for j in range(1, 4):
            arrived(block(j, 1, x), sent, got, 4 + j, z_peer(j))
            to_x(j, 1)
            to_core(j, 0, x)
        yield
        for j in range(4):
            theirs = block(j, 1, right)
            arrived(theirs, sent, got, 17 + 2 * j, x_peer(1))
            send(theirs, theirs, sent, got, 25 + 2 * j, x_peer(3))
            arrived(block(j, 1, left), sent, got, 9 + 2 * j, x_peer(3))
            to_core(j, 1, left)
            to_core(j, 2, right)
        yield
        for j in range(4):
            arrived(block(j, 0, beyond), sent, got, 24 + 2 * j, x_peer(3))
            arrived(block(j, 1, beyond), sent, got, 25 + 2 * j, x_peer(1))
            to_core(j, 3, beyond)
        yield
        for n, xx in enumerate((x, left, right, beyond)):
            for j in range(4):
                arrived(buf.at[:, low(j), xx, 1 - c], sent, got, 32 + 4 * n + j, core_peer)
        yield

    def project(a):
        sent, got = proj_sent.at[a], proj_got.at[a]
        head = heads[a].reshape(features.shape[2], 128)
        proj = jnp.dot(features[a], head, preferred_element_type=F32)
        proj_own[a] = proj
        projs[a, half, y] = proj.astype(LOW)
        mine, other = projs.at[a, half, y], projs.at[a, 1 - half, y]
        send(mine, mine, sent, got, 0, half_peer)
        for k in (2, 1, 3):
            send(mine, mine, sent, got, k, y_peer(k))
        yield
        arrived(other, sent, got, 0, half_peer)
        for k in (2, 1, 3):
            send(other, other, sent, got, 4 + k, y_peer(k))
        yield
        for k in range(1, 4):
            arrived(projs.at[a, half, y_left(k)], sent, got, k, y_peer(k))
        for k in range(1, 4):
            arrived(projs.at[a, 1 - half, y_left(k)], sent, got, 4 + k, y_peer(k))
        yield

    def normalised(a, rows):
        parts = [projs[a, t // NY, t % NY, rows, :].astype(F32) for t in range(8)]
        squares = parts[0] * parts[0]
        for part in parts[1:]:
            squares = squares + part * part
        scale = lax.rsqrt(jnp.sum(squares, axis=1, keepdims=True) + EPS)
        return scale, [(part * scale).astype(LOW) for part in parts]

    def first_units(a):
        _, rounded = normalised(a, pl.ds(pl.multiple_of(tensor * 16, 16), 16))
        for t in range(8):
            pairs[a, high(0), low(0), x, c, :, t * 128:(t + 1) * 128] = rounded[t]

    def all_units(a):
        scale, rounded = normalised(a, slice(None))
        inverse[a] = jnp.broadcast_to(scale, (128, 128))
        for t in range(8):
            units[a, :, t * 128:(t + 1) * 128] = rounded[t]

    def embed(a):
        sent, got = d_sent.at[a], d_got.at[a]
        factor = SCALE * loss_grad[0] / total
        minus_sign = jnp.where(own_ids[...] == pair_ids[...], -1.0, 1.0).astype(F32)
        others = pairs[1 - a].reshape(1024, 1024)
        summed = lax.dot_general(units[a], others, NT, preferred_element_type=F32)
        logit = SCALE * summed + BIAS
        weights = (factor * minus_sign * jax.nn.sigmoid(minus_sign * logit)).astype(LOW)
        dot = jnp.sum(weights.astype(F32) * summed, axis=1, keepdims=True)
        d = jnp.dot(weights, others, preferred_element_type=F32)
        for t in range(8):
            piece = d[:, t * 128:(t + 1) * 128]
            d_own[a, t // NY, t % NY] = piece
            d_send[a, t // NY, t % NY] = piece.astype(LOW)
        dots[a, 0] = jnp.transpose(jnp.broadcast_to(dot, (128, 128)))[:8]
        for k in (2, 1, 3):
            send(d_send.at[a, 1 - half, y_right(k)], d_recv.at[a, 0, k], sent, got, k, y_peer(k))
            send(dots.at[a, 0], dots.at[a, k], sent, got, 4 + k, y_peer(k))
        for k in (2, 1, 3):
            send(d_send.at[a, half, y_right(k)], d_recv.at[a, 1, k], sent, got, 8 + k, y_peer(k))
        yield
        away = d_own[a, 1 - half, y]
        for k in range(1, 4):
            arrived(d_recv.at[a, 0, k], sent, got, k, y_peer(k))
            away = away + d_recv[a, 0, k].astype(F32)
        d_last[a, 0] = away.astype(LOW)
        send(d_last.at[a, 0], d_last.at[a, 1], sent, got, 0, half_peer)
        for k in range(1, 4):
            arrived(dots.at[a, k], sent, got, 4 + k, y_peer(k))
        dots[a, 4] = dots[a, 0] + dots[a, 1] + dots[a, 2] + dots[a, 3]
        send(dots.at[a, 4], dots.at[a, 5], sent, got, 4, half_peer)
        yield
        d = d_own[a, half, y]
        for k in range(1, 4):
            arrived(d_recv.at[a, 1, k], sent, got, 8 + k, y_peer(k))
            d = d + d_recv[a, 1, k].astype(F32)
        arrived(d_last.at[a, 1], sent, got, 0, half_peer)
        arrived(dots.at[a, 5], sent, got, 4, half_peer)
        d = d + d_last[a, 1].astype(F32)
        dot = jnp.transpose(jnp.broadcast_to((dots[a, 4] + dots[a, 5])[:1], (128, 128)))
        scale = inverse[a]
        grad = ((d - proj_own[a] * scale * dot) * scale).astype(LOW)

        sent, got = grad_sent.at[a], grad_got.at[a]
        for k in (2, 1, 3, 0):
            for zz in range(8):
                columns = pl.ds(pl.multiple_of((zz * NX + x_right(k)) * 128, 128), 128)
                part = lax.dot_general(features[a, :, columns], grad, TN, preferred_element_type=F32)
                part = part.reshape(2, 64, 128)
                first, second = part[0], part[1]
                own_part[a, k, zz // 4, zz % 4] = jnp.where(c == 0, first, second)
                core_send[a, k, zz // 4, zz % 4] = jnp.where(c == 0, second, first).astype(LOW)
            send(core_send.at[a, k], core_recv.at[a, k], sent, got, k, core_peer)
        yield
        for k in (2, 1, 3):
            arrived(core_recv.at[a, k], sent, got, k, core_peer)
            x_send[a, k] = (own_part[a, k] + core_recv[a, k].astype(F32)).astype(LOW)
            send(x_send.at[a, k], x_recv.at[a, k], sent, got, 4 + k, x_peer(k))
        arrived(core_recv.at[a, 0], sent, got, 0, core_peer)
        z_own[a] = own_part[a, 0] + core_recv[a, 0].astype(F32)
        yield
        for k in (1, 3, 2):
            arrived(x_recv.at[a, k], sent, got, 4 + k, x_peer(k))
        summed = z_own[a]
        for k in (1, 2, 3):
            summed = summed + x_recv[a, k].astype(F32)
        z_own[a] = summed
        z_send[a] = summed.astype(LOW)
        for k in (7, 6, 5, 4, 3, 2, 1):
            there = z_send.at[a, high(k // 4), low(k % 4)]
            send(there, z_recv.at[a, k], sent, got, 8 + k, z_peer(k))
        yield
        done = z_own[a, high(0), low(0)]
        for k in range(1, 8):
            arrived(z_recv.at[a, k], sent, got, 8 + k, z_peer(k))
            done = done + z_recv[a, k].astype(F32)
        (visit_out, note_out)[a][...] = done
        yield

    loads = [
        pltpu.make_async_copy(src, dst, load_done.at[n])
        for n, (src, dst) in enumerate((
            (visit_weight, heads.at[0, high(0), low(0), x, c]),
            (note_weight, heads.at[1, high(0), low(0), x, c]),
            (visits_in, features.at[0]),
            (notes_in, features.at[1]),
        ))
    ]
    for load in loads:
        load.start()
    loads[0].wait()
    loads[1].wait()
    pl.semaphore_wait(barrier, len(peers))

    ga, gb = [gather(heads.at[a], head_sent.at[a], head_got.at[a]) for a in range(2)]
    for _ in range(7):
        next(ga)
        next(gb)
    pa, pb = project(0), project(1)
    loads[2].wait()
    next(ga)
    next(pa)
    loads[3].wait()
    next(gb)
    next(pb)
    next(pa)
    next(pb)
    ga, gb = [gather(pairs.at[a], pair_sent.at[a], pair_got.at[a]) for a in range(2)]
    next(pa)
    first_units(0)
    next(ga)
    next(pb)
    first_units(1)
    next(gb)
    all_units(1)
    next(ga)
    all_units(0)
    ea, eb = embed(0), embed(1)
    order = (
        ga, gb, ga, gb, ga, gb, ga, gb, ga, gb, ga,
        eb, gb, eb, gb, ea, ea, eb, ea, eb, eb, ea, ea, eb, ea,
    )
    for step in order:
        next(step)
    for copy in started:
        copy.wait_send()


def local(visits, notes, visit_weight, note_weight, patient_ids, loss_grad):
    rows = visits.shape[0]
    total = patient_ids.shape[0]
    dp, tensor = lax.axis_index("dp"), lax.axis_index("tensor")
    own_ids = lax.dynamic_slice_in_dim(patient_ids, dp * rows, rows, 0).reshape(rows, 1)
    pair_ids = lax.dynamic_slice_in_dim(
        patient_ids.reshape(total // rows, rows), tensor * 16, 16, 1
    ).reshape(1, -1)
    vmem = pl.BlockSpec(memory_space=pltpu.VMEM)
    hbm = pl.BlockSpec(memory_space=pl.ANY)
    grad = jax.ShapeDtypeStruct(visit_weight.shape, F32)
    sems = pltpu.SemaphoreType.DMA
    return pl.pallas_call(
        functools.partial(kernel, total),
        out_shape=(grad, grad),
        in_specs=[hbm] * 4 + [vmem] * 2 + [pl.BlockSpec(memory_space=pltpu.SMEM)],
        out_specs=(vmem, vmem),
        scratch_shapes=[
            pltpu.VMEM((2,) + visits.shape, LOW),
            pltpu.VMEM((2, 2, 4, 4, 2, 64, 128), LOW),
            pltpu.VMEM((2, 2, 4, 128, 128), LOW),
            pltpu.VMEM((2, 128, 128), F32),
            pltpu.VMEM((2, 128, 128), F32),
            pltpu.VMEM((2, 128, 1024), LOW),
            pltpu.VMEM((2, 2, 4, 4, 2, 16, 1024), LOW),
            pltpu.VMEM((2, 2, 4, 128, 128), F32),
            pltpu.VMEM((2, 2, 4, 128, 128), LOW),
            pltpu.VMEM((2, 2, 4, 128, 128), LOW),
            pltpu.VMEM((2, 2, 128, 128), LOW),
            pltpu.VMEM((2, 6, 8, 128), F32),
            pltpu.VMEM((2, 4, 2, 4, 64, 128), F32),
            pltpu.VMEM((2, 4, 2, 4, 64, 128), LOW),
            pltpu.VMEM((2, 4, 2, 4, 64, 128), LOW),
            pltpu.VMEM((2, 4, 2, 4, 64, 128), LOW),
            pltpu.VMEM((2, 4, 2, 4, 64, 128), LOW),
            pltpu.VMEM((2, 2, 4, 64, 128), F32),
            pltpu.VMEM((2, 2, 4, 64, 128), LOW),
            pltpu.VMEM((2, 8, 64, 128), LOW),
            sems((4,)),
            sems((2, 48)), sems((2, 48)),
            sems((2, 8)), sems((2, 8)),
            sems((2, 48)), sems((2, 48)),
            sems((2, 12)), sems((2, 12)),
            sems((2, 16)), sems((2, 16)),
        ],
        compiler_params=pltpu.CompilerParams(
            collective_id=0, has_side_effects=True, vmem_limit_bytes=48 * 1024 * 1024
        ),
    )(visits, notes, visit_weight, note_weight, own_ids, pair_ids, loss_grad)


def solution(mesh):
    return jax.shard_map(
        local,
        mesh=mesh,
        in_specs=(P("dp", None), P("dp", None), P("dp", "tensor"), P("dp", "tensor"), P(), P()),
        out_specs=(P("dp", "tensor"), P("dp", "tensor")),
        check_vma=False,
    )
```

```python
import functools

import jax
import jax.numpy as jnp
from jax import lax
from jax.experimental import pallas as pl
from jax.experimental.pallas import tpu as pltpu
from jax.sharding import PartitionSpec as P

SCALE = 10.0
BIAS = -2.0
EPS = 1e-06
F32 = jnp.float32
LOW = jnp.bfloat16
NT = (((1,), (1,)), ((), ()))
TN = (((0,), (0,)), ((), ()))
NX, NY = 4, 4
FAR_DIRECT = False
DOUBLING = False
ORDER = ('abababababababab', 'abab', 'aababuwababab', 'aBbBb', 'AABBAABBAABA')


def flip(value, bit):
    return 1 - value if bit else value


def kernel(
    total,
    visits_in, notes_in, visit_weight, note_weight, ids_in, loss_grad,
    visit_out, note_out,
    ids, moved, signs, features, heads, projs, proj_own, inverse, units, pairs,
    d_own, d_send, d_recv, d_last, dots,
    own_part, core_send, core_recv, x_send, x_recv, z_own, z_send, z_recv,
    load_done, head_sent, head_got, proj_sent, proj_got, pair_sent, pair_got,
    d_sent, d_got, grad_sent, grad_got,
):
    dp, tensor = lax.axis_index("dp"), lax.axis_index("tensor")
    c, x, z = lax.rem(dp, 2), lax.rem(lax.div(dp, 2), NX), lax.div(dp, 2 * NX)
    z0, z1, z2 = lax.rem(z, 2), lax.rem(lax.div(z, 2), 2), lax.div(z, 4)
    y, half = lax.rem(tensor, NY), lax.div(tensor, NY)
    left, right = lax.rem(x + NX - 1, NX), lax.rem(x + 1, NX)
    beyond = lax.rem(x + 2, NX)

    def low(j):
        return flip(z1, j // 2) * 2 + flip(z0, j % 2)

    def high(f):
        return flip(z2, f)

    def at(zz, xx, cc):
        return ((zz * NX + xx) * 2 + cc, tensor)

    def z_peer(k):
        return at(high(k // 4) * 4 + low(k % 4), x, c)

    def x_right(k):
        return lax.rem(x + k, NX)

    def x_peer(k):
        return at(z, x_right(k), c)

    def y_right(k):
        return lax.rem(y + k, NY)

    def y_left(k):
        return lax.rem(y + NY - k, NY)

    def y_peer(k):
        return (dp, half * NY + y_right(k))

    core_peer = at(z, x, 1 - c)
    half_peer = (dp, (1 - half) * NY + y)
    middle_peer = (((1 - z2) * 4 + low(0)) * NX * 2 + x * 2 + c, (1 - half) * NY + y)

    started = []

    def send(src, dst, sent, got, n, peer):
        copy = pltpu.make_async_remote_copy(
            src_ref=src, dst_ref=dst, send_sem=sent.at[n], recv_sem=got.at[n],
            device_id=peer, device_id_type=pl.DeviceIdType.MESH,
        )
        copy.start()
        started.append(copy)

    def arrived(dst, sent, got, n, peer):
        pltpu.make_async_remote_copy(
            src_ref=dst, dst_ref=dst, send_sem=sent.at[n], recv_sem=got.at[n],
            device_id=peer, device_id_type=pl.DeviceIdType.MESH,
        ).wait_recv()

    peers = (
        [z_peer(k) for k in range(1, 5)] + [x_peer(k) for k in range(1, 4)]
        + [y_peer(k) for k in range(1, 4)] + [core_peer, middle_peer]
    )
    barrier = pltpu.get_barrier_semaphore()
    for peer in peers:
        pl.semaphore_signal(barrier, inc=1, device_id=peer, device_id_type=pl.DeviceIdType.MESH)

    def gather(buf, sent, got):
        def block(j, f, xx):
            return buf.at[high(f), low(j), xx, c]

        def to_z(j, f, peer, n):
            here = block(j, f, x)
            send(here, here, sent, got, 4 * f + n, z_peer(peer))

        def from_z(j, f, peer):
            arrived(block(j, f, x), sent, got, 4 * f + j, z_peer(peer))

        def to_x(j, f):
            here = block(j, f, x)
            send(here, here, sent, got, 8 + 2 * j + f, x_peer(1))
            send(here, here, sent, got, 16 + 2 * j + f, x_peer(3))
            if f and FAR_DIRECT:
                send(here, here, sent, got, 24 + 2 * j + f, x_peer(2))

        def to_core(j, n, xx):
            chunk = buf.at[:, low(j), xx, c]
            send(chunk, chunk, sent, got, 32 + 4 * n + j, core_peer)

        mine = block(0, 0, x)
        send(mine, mine, sent, got, 0, z_peer(4))
        for j in (2, 1) if DOUBLING else (3, 2, 1):
            to_z(0, 0, j, j)
        to_x(0, 0)
        yield
        for j in (2, 1, 3) if DOUBLING else (1, 2, 3):
            from_z(j, 0, 1 if DOUBLING and j == 3 else j)
            if DOUBLING and j == 2:
                to_z(2, 0, 1, 3)
            to_x(j, 0)
        yield
        arrived(block(0, 1, x), sent, got, 0, z_peer(4))
        for j in (2, 1) if DOUBLING else (3, 2, 1):
            to_z(0, 1, j, j)
        to_x(0, 1)
        to_core(0, 0, x)
        yield
        for j in range(4):
            theirs = block(j, 0, left)
            arrived(theirs, sent, got, 8 + 2 * j, x_peer(3))
            send(theirs, theirs, sent, got, 24 + 2 * j, x_peer(1))
            arrived(block(j, 0, right), sent, got, 16 + 2 * j, x_peer(1))
        yield
        for j in (2, 1, 3):
            from_z(j, 1, 1 if DOUBLING and j == 3 else j)
            if DOUBLING and j == 2:
                to_z(2, 1, 1, 3)
            to_x(j, 1)
            to_core(j, 0, x)
        yield
        for j in (0, 2, 1, 3):
            theirs = block(j, 1, right)
            arrived(theirs, sent, got, 17 + 2 * j, x_peer(1))
            if not FAR_DIRECT:
                send(theirs, theirs, sent, got, 25 + 2 * j, x_peer(3))
            arrived(block(j, 1, left), sent, got, 9 + 2 * j, x_peer(3))
            to_core(j, 1, left)
            to_core(j, 2, right)
        yield
        for j in (0, 2, 1, 3):
            arrived(block(j, 0, beyond), sent, got, 24 + 2 * j, x_peer(3))
            arrived(block(j, 1, beyond), sent, got, 25 + 2 * j, x_peer(1))
            to_core(j, 3, beyond)
        yield
        for n, xx in enumerate((x, left, right, beyond)):
            for j in range(4):
                arrived(buf.at[:, low(j), xx, 1 - c], sent, got, 32 + 4 * n + j, core_peer)

    def project(a):
        sent, got = proj_sent.at[a], proj_got.at[a]
        head = heads[a].reshape(features.shape[2], 128)
        proj = jnp.dot(features[a], head, preferred_element_type=F32)
        proj_own[a] = proj
        projs[a, half, y] = proj.astype(LOW)
        mine, other = projs.at[a, half, y], projs.at[a, 1 - half, y]
        send(mine, mine, sent, got, 0, half_peer)
        for k in (2, 1, 3):
            send(mine, mine, sent, got, k, y_peer(k))
        yield
        arrived(other, sent, got, 0, half_peer)
        for k in (2, 1, 3):
            send(other, other, sent, got, 4 + k, y_peer(k))
        yield
        for k in range(1, 4):
            arrived(projs.at[a, half, y_left(k)], sent, got, k, y_peer(k))
        for k in range(1, 4):
            arrived(projs.at[a, 1 - half, y_left(k)], sent, got, 4 + k, y_peer(k))

    def normalised(a, rows):
        parts = [projs[a, t // NY, t % NY, rows, :].astype(F32) for t in range(8)]
        squares = parts[0] * parts[0]
        for part in parts[1:]:
            squares = squares + part * part
        scale = lax.rsqrt(jnp.sum(squares, axis=1, keepdims=True) + EPS)
        return scale, [(part * scale).astype(LOW) for part in parts]

    def first_units(a):
        _, rounded = normalised(a, pl.ds(pl.multiple_of(tensor * 16, 16), 16))
        for t in range(8):
            pairs[a, high(0), low(0), x, c, :, t * 128:(t + 1) * 128] = rounded[t]

    def all_units(a):
        scale, rounded = normalised(a, slice(None))
        inverse[a] = jnp.broadcast_to(scale, (128, 128))
        for t in range(8):
            units[a, :, t * 128:(t + 1) * 128] = rounded[t]

    def embed(a):
        sent, got = d_sent.at[a], d_got.at[a]
        factor = SCALE * loss_grad[0] / total
        minus_sign = signs[...]
        others = pairs[1 - a].reshape(1024, 1024)
        summed = lax.dot_general(units[a], others, NT, preferred_element_type=F32)
        logit = SCALE * summed + BIAS
        weights = (factor * minus_sign * jax.nn.sigmoid(minus_sign * logit)).astype(LOW)
        dot = jnp.sum(weights.astype(F32) * summed, axis=1, keepdims=True)
        d = jnp.dot(weights, others, preferred_element_type=F32)
        for t in range(8):
            piece = d[:, t * 128:(t + 1) * 128]
            d_own[a, t // NY, t % NY] = piece
            d_send[a, t // NY, t % NY] = piece.astype(LOW)
        dots[a, 0] = jnp.transpose(jnp.broadcast_to(dot, (128, 128)))[:8]
        for k in (2, 1, 3):
            send(d_send.at[a, 1 - half, y_right(k)], d_recv.at[a, 0, k], sent, got, k, y_peer(k))
            send(dots.at[a, 0], dots.at[a, k], sent, got, 4 + k, y_peer(k))
        for k in (2, 1, 3):
            send(d_send.at[a, half, y_right(k)], d_recv.at[a, 1, k], sent, got, 8 + k, y_peer(k))
        yield
        away = d_own[a, 1 - half, y]
        for k in range(1, 4):
            arrived(d_recv.at[a, 0, k], sent, got, k, y_peer(k))
            away = away + d_recv[a, 0, k].astype(F32)
        d_last[a, 0] = away.astype(LOW)
        send(d_last.at[a, 0], d_last.at[a, 1], sent, got, 0, half_peer)
        for k in range(1, 4):
            arrived(dots.at[a, k], sent, got, 4 + k, y_peer(k))
        dots[a, 4] = dots[a, 0] + dots[a, 1] + dots[a, 2] + dots[a, 3]
        send(dots.at[a, 4], dots.at[a, 5], sent, got, 4, half_peer)
        yield
        d = d_own[a, half, y]
        for k in range(1, 4):
            arrived(d_recv.at[a, 1, k], sent, got, 8 + k, y_peer(k))
            d = d + d_recv[a, 1, k].astype(F32)
        arrived(d_last.at[a, 1], sent, got, 0, half_peer)
        arrived(dots.at[a, 5], sent, got, 4, half_peer)
        d = d + d_last[a, 1].astype(F32)
        dot = jnp.transpose(jnp.broadcast_to((dots[a, 4] + dots[a, 5])[:1], (128, 128)))
        scale = inverse[a]
        grad = ((d - proj_own[a] * scale * dot) * scale).astype(LOW)

        sent, got = grad_sent.at[a], grad_got.at[a]
        for k in (2, 1, 3, 0):
            for zz in range(8):
                columns = pl.ds(pl.multiple_of((zz * NX + x_right(k)) * 128, 128), 128)
                part = lax.dot_general(features[a, :, columns], grad, TN, preferred_element_type=F32)
                part = part.reshape(2, 64, 128)
                first, second = part[0], part[1]
                own_part[a, k, zz // 4, zz % 4] = jnp.where(c == 0, first, second)
                core_send[a, k, zz // 4, zz % 4] = jnp.where(c == 0, second, first).astype(LOW)
            send(core_send.at[a, k], core_recv.at[a, k], sent, got, k, core_peer)
        yield
        for f in (1, 0):
            to = high(f)
            for k in (2, 1, 3):
                if f:
                    arrived(core_recv.at[a, k], sent, got, k, core_peer)
                x_send[a, k, to] = (own_part[a, k, to] + core_recv[a, k, to].astype(F32)).astype(LOW)
                n = 4 * (2 - f) + k
                send(x_send.at[a, k, to], x_recv.at[a, k, to], sent, got, n, x_peer(k))
        arrived(core_recv.at[a, 0], sent, got, 0, core_peer)
        z_own[a] = own_part[a, 0] + core_recv[a, 0].astype(F32)
        yield
        for f in (1, 0):
            to = high(f)
            summed = z_own[a, to]
            for k in (1, 3, 2):
                arrived(x_recv.at[a, k, to], sent, got, 4 * (2 - f) + k, x_peer(k))
                summed = summed + x_recv[a, k, to].astype(F32)
            z_own[a, to] = summed
            z_send[a, to] = summed.astype(LOW)
            for k in ((7, 6, 5, 4) if f else (3, 2, 1)):
                there = z_send.at[a, to, low(k % 4)]
                send(there, z_recv.at[a, k], sent, got, 12 + k, z_peer(k))
            if f:
                yield
        yield
        done = z_own[a, high(0), low(0)]
        for k in range(1, 8):
            arrived(z_recv.at[a, k], sent, got, 12 + k, z_peer(k))
            done = done + z_recv[a, k].astype(F32)
        (visit_out, note_out)[a][...] = done
        yield

    def mark_signs():
        own = jnp.transpose(jnp.broadcast_to(ids[pl.ds(dp, 1), :], (128, 128)))
        moved[...] = pltpu.roll(ids[...], lax.rem(128 - tensor * 16, 128), 1)
        lane = lax.div(lax.broadcasted_iota(jnp.int32, (8, 128), 1), 16)
        packed = jnp.zeros((8, 128), jnp.int32)
        for k in range(8):
            part = moved[pl.ds(k, 8, stride=8), :]
            packed = jnp.where(lane == k, pltpu.roll(part, 16 * k, 1) if k else part, packed)
        for n in range(8):
            row = packed[n:n + 1]
            signs[:, n * 128:(n + 1) * 128] = jnp.where(own == row, -1.0, 1.0).astype(F32)

    def chain(a):
        yield from gather(heads.at[a], head_sent.at[a], head_got.at[a])
        loads[2 + a].wait()
        yield from project(a)
        first_units(a)
        yield from gather(pairs.at[a], pair_sent.at[a], pair_got.at[a])
        yield

    loads = [
        pltpu.make_async_copy(src, dst, load_done.at[n])
        for n, (src, dst) in enumerate((
            (visit_weight, heads.at[0, high(0), low(0), x, c]),
            (note_weight, heads.at[1, high(0), low(0), x, c]),
            (visits_in, features.at[0]),
            (notes_in, features.at[1]),
            (ids_in, ids),
        ))
    ]
    for n in (4, 0, 1, 2, 3):
        loads[n].start()
    loads[4].wait()
    mark_signs()
    loads[0].wait()
    loads[1].wait()
    pl.semaphore_wait(barrier, len(peers))

    steps = {"a": chain(0), "b": chain(1), "A": embed(0), "B": embed(1)}
    for step in "".join(ORDER):
        if step in "uw":
            all_units("uw".index(step))
        else:
            next(steps[step])
    for copy in started:
        copy.wait_send()


def local(visits, notes, visit_weight, note_weight, patient_ids, loss_grad):
    rows = visits.shape[0]
    total = patient_ids.shape[0]
    vmem = pl.BlockSpec(memory_space=pltpu.VMEM)
    hbm = pl.BlockSpec(memory_space=pltpu.HBM)
    grad = jax.ShapeDtypeStruct(visit_weight.shape, F32)
    sems = pltpu.SemaphoreType.DMA
    return pl.pallas_call(
        functools.partial(kernel, total),
        out_shape=(grad, grad),
        in_specs=[hbm] * 5 + [pl.BlockSpec(memory_space=pltpu.SMEM)],
        out_specs=(vmem, vmem),
        scratch_shapes=[
            pltpu.VMEM((total // rows, rows), jnp.int32),
            pltpu.VMEM((total // rows, rows), jnp.int32),
            pltpu.VMEM((128, 1024), F32),
            pltpu.VMEM((2,) + visits.shape, LOW),
            pltpu.VMEM((2, 2, 4, 4, 2, 64, 128), LOW),
            pltpu.VMEM((2, 2, 4, 128, 128), LOW),
            pltpu.VMEM((2, 128, 128), F32),
            pltpu.VMEM((2, 128, 128), F32),
            pltpu.VMEM((2, 128, 1024), LOW),
            pltpu.VMEM((2, 2, 4, 4, 2, 16, 1024), LOW),
            pltpu.VMEM((2, 2, 4, 128, 128), F32),
            pltpu.VMEM((2, 2, 4, 128, 128), LOW),
            pltpu.VMEM((2, 2, 4, 128, 128), LOW),
            pltpu.VMEM((2, 2, 128, 128), LOW),
            pltpu.VMEM((2, 6, 8, 128), F32),
            pltpu.VMEM((2, 4, 2, 4, 64, 128), F32),
            pltpu.VMEM((2, 4, 2, 4, 64, 128), LOW),
            pltpu.VMEM((2, 4, 2, 4, 64, 128), LOW),
            pltpu.VMEM((2, 4, 2, 4, 64, 128), LOW),
            pltpu.VMEM((2, 4, 2, 4, 64, 128), LOW),
            pltpu.VMEM((2, 2, 4, 64, 128), F32),
            pltpu.VMEM((2, 2, 4, 64, 128), LOW),
            pltpu.VMEM((2, 8, 64, 128), LOW),
            sems((5,)),
            sems((2, 48)), sems((2, 48)),
            sems((2, 8)), sems((2, 8)),
            sems((2, 48)), sems((2, 48)),
            sems((2, 12)), sems((2, 12)),
            sems((2, 20)), sems((2, 20)),
        ],
        compiler_params=pltpu.CompilerParams(
            collective_id=0, has_side_effects=True, vmem_limit_bytes=60 * 1024 * 1024
        ),
    )(visits, notes, visit_weight, note_weight, patient_ids.reshape(-1, rows), loss_grad)


def solution(mesh):
    return jax.shard_map(
        local,
        mesh=mesh,
        in_specs=(P("dp", None), P("dp", None), P("dp", "tensor"), P("dp", "tensor"), P(), P()),
        out_specs=(P("dp", "tensor"), P("dp", "tensor")),
        check_vma=False,
    )
```

```python
import functools

import jax
import jax.numpy as jnp
from jax import lax
from jax.experimental import pallas as pl
from jax.experimental.pallas import tpu as pltpu
from jax.sharding import PartitionSpec as P

SCALE = 10.0
BIAS = -2.0
EPS = 1e-06
F32 = jnp.float32
LOW = jnp.bfloat16
NT = (((1,), (1,)), ((), ()))
TN = (((0,), (0,)), ((), ()))
NX, NY = 4, 4
ORDER = ('aabababababababb', 'cdab', 'aabcdabababdab', 'aBbBbc', 'AABBAABBAABA')


def flip(value, bit):
    return 1 - value if bit else value


def kernel(
    total,
    visits_in, notes_in, visit_weight, note_weight, ids_in, loss_grad,
    visit_out, note_out,
    ids, moved, signs, features, heads, projs, firsts, proj_own, inverse, units, pairs,
    d_own, d_send, d_recv, d_last, dots,
    own_part, core_send, core_recv, x_send, x_recv, z_own, z_send, z_recv,
    load_done, head_sent, head_got, proj_sent, proj_got, pair_sent, pair_got,
    d_sent, d_got, grad_sent, grad_got, known,
):
    dp, tensor = lax.axis_index("dp"), lax.axis_index("tensor")
    c, x, z = lax.rem(dp, 2), lax.rem(lax.div(dp, 2), NX), lax.div(dp, 2 * NX)
    z0, z1, z2 = lax.rem(z, 2), lax.rem(lax.div(z, 2), 2), lax.div(z, 4)
    y, half = lax.rem(tensor, NY), lax.div(tensor, NY)
    left, right = lax.rem(x + NX - 1, NX), lax.rem(x + 1, NX)
    beyond = lax.rem(x + 2, NX)

    def low(j):
        return flip(z1, j // 2) * 2 + flip(z0, j % 2)

    def high(f):
        return flip(z2, f)

    def at(zz, xx, cc):
        return ((zz * NX + xx) * 2 + cc, tensor)

    def z_peer(k):
        return at(high(k // 4) * 4 + low(k % 4), x, c)

    def x_right(k):
        return lax.rem(x + k, NX)

    def x_peer(k):
        return at(z, x_right(k), c)

    def y_right(k):
        return lax.rem(y + k, NY)

    def y_left(k):
        return lax.rem(y + NY - k, NY)

    def y_peer(k):
        return (dp, half * NY + y_right(k))

    core_peer = at(z, x, 1 - c)
    half_peer = (dp, (1 - half) * NY + y)
    middle_peer = (((1 - z2) * 4 + low(0)) * NX * 2 + x * 2 + c, (1 - half) * NY + y)

    started = []

    def send(src, dst, sent, got, n, peer):
        copy = pltpu.make_async_remote_copy(
            src_ref=src, dst_ref=dst, send_sem=sent.at[n], recv_sem=got.at[n],
            device_id=peer, device_id_type=pl.DeviceIdType.MESH,
        )
        copy.start()
        started.append(copy)

    def arrived(dst, sent, got, n, peer):
        pltpu.make_async_remote_copy(
            src_ref=dst, dst_ref=dst, send_sem=sent.at[n], recv_sem=got.at[n],
            device_id=peer, device_id_type=pl.DeviceIdType.MESH,
        ).wait_recv()

    peers = (
        [z_peer(k) for k in range(1, 5)] + [x_peer(k) for k in range(1, 4)]
        + [y_peer(k) for k in range(1, 4)] + [core_peer, middle_peer]
    )
    barrier = pltpu.get_barrier_semaphore()
    for peer in peers:
        pl.semaphore_signal(barrier, inc=1, device_id=peer, device_id_type=pl.DeviceIdType.MESH)

    def gather(buf, sent, got):
        def block(j, f, xx):
            return buf.at[high(f), low(j), xx, c]

        def to_z(j, f, peer, n):
            here = block(j, f, x)
            send(here, here, sent, got, 4 * f + n, z_peer(peer))

        def from_z(j, f, peer):
            arrived(block(j, f, x), sent, got, 4 * f + j, z_peer(peer))

        def to_x(j, f):
            here = block(j, f, x)
            send(here, here, sent, got, 8 + 2 * j + f, x_peer(1))
            send(here, here, sent, got, 16 + 2 * j + f, x_peer(3))

        def to_core(j, n, xx):
            chunk = buf.at[:, low(j), xx, c]
            send(chunk, chunk, sent, got, 32 + 4 * n + j, core_peer)

        mine = block(0, 0, x)
        send(mine, mine, sent, got, 0, z_peer(4))
        for j in (3, 2, 1):
            to_z(0, 0, j, j)
        to_x(0, 0)
        yield
        for j in (1, 2, 3):
            from_z(j, 0, j)
            to_x(j, 0)
        yield
        arrived(block(0, 1, x), sent, got, 0, z_peer(4))
        for j in (3, 2, 1):
            to_z(0, 1, j, j)
        to_x(0, 1)
        to_core(0, 0, x)
        yield
        for j in range(4):
            theirs = block(j, 0, left)
            arrived(theirs, sent, got, 8 + 2 * j, x_peer(3))
            send(theirs, theirs, sent, got, 24 + 2 * j, x_peer(1))
            arrived(block(j, 0, right), sent, got, 16 + 2 * j, x_peer(1))
        yield
        for j in (2, 1, 3):
            from_z(j, 1, j)
            to_x(j, 1)
            to_core(j, 0, x)
        yield
        for j in (0, 2, 1, 3):
            theirs = block(j, 1, right)
            arrived(theirs, sent, got, 17 + 2 * j, x_peer(1))
            send(theirs, theirs, sent, got, 25 + 2 * j, x_peer(3))
            arrived(block(j, 1, left), sent, got, 9 + 2 * j, x_peer(3))
            to_core(j, 1, left)
            to_core(j, 2, right)
        yield
        for j in (0, 2, 1, 3):
            arrived(block(j, 0, beyond), sent, got, 24 + 2 * j, x_peer(3))
            arrived(block(j, 1, beyond), sent, got, 25 + 2 * j, x_peer(1))
            to_core(j, 3, beyond)
        yield
        for n, xx in enumerate((x, left, right, beyond)):
            for j in range(4):
                arrived(buf.at[:, low(j), xx, 1 - c], sent, got, 32 + 4 * n + j, core_peer)

    def project(a):
        sent, got = proj_sent.at[a], proj_got.at[a]
        head = heads[a].reshape(features.shape[2], 128)
        proj = jnp.dot(features[a], head, preferred_element_type=F32)
        proj_own[a] = proj
        projs[a, half, y] = proj.astype(LOW)
        if a == 0:
            pl.semaphore_wait(known, 3)
        for f in (1, 0):
            for k in (2, 1, 3, 0):
                peer = flip(half, f) * NY + y_right(k)
                part = projs.at[a, half, y, pl.ds(pl.multiple_of(peer * 16, 16), 16)]
                if f or k:
                    send(part, firsts.at[a, half, y], sent, got, 8 + 4 * f + k, (dp, peer))
        firsts[a, half, y] = projs[a, half, y, pl.ds(pl.multiple_of(tensor * 16, 16), 16), :]
        yield
        for f in (0, 1):
            for k in range(4):
                if f or k:
                    peer = flip(half, f) * NY + y_right(k)
                    slot = firsts.at[a, flip(half, f), y_left(k)]
                    arrived(slot, sent, got, 8 + 4 * f + k, (dp, peer))
        _, rounded = normalised([firsts[a, t // NY, t % NY] for t in range(8)])
        for t in range(8):
            pairs[a, high(0), low(0), x, c, :, t * 128:(t + 1) * 128] = rounded[t]

    def spread(a):
        sent, got = proj_sent.at[a], proj_got.at[a]
        mine, other = projs.at[a, half, y], projs.at[a, 1 - half, y]
        send(mine, mine, sent, got, 0, half_peer)
        for k in (2, 1, 3):
            send(mine, mine, sent, got, k, y_peer(k))
        yield
        arrived(other, sent, got, 0, half_peer)
        for k in (2, 1, 3):
            send(other, other, sent, got, 4 + k, y_peer(k))
        yield
        for k in range(1, 4):
            arrived(projs.at[a, half, y_left(k)], sent, got, k, y_peer(k))
        for k in range(1, 4):
            arrived(projs.at[a, 1 - half, y_left(k)], sent, got, 4 + k, y_peer(k))
        scale, rounded = normalised([projs[a, t // NY, t % NY] for t in range(8)])
        inverse[a] = jnp.broadcast_to(scale, (128, 128))
        for t in range(8):
            units[a, :, t * 128:(t + 1) * 128] = rounded[t]
        yield

    def normalised(parts):
        parts = [part.astype(F32) for part in parts]
        squares = parts[0] * parts[0]
        for part in parts[1:]:
            squares = squares + part * part
        scale = lax.rsqrt(jnp.sum(squares, axis=1, keepdims=True) + EPS)
        return scale, [(part * scale).astype(LOW) for part in parts]

    def embed(a):
        sent, got = d_sent.at[a], d_got.at[a]
        factor = SCALE * loss_grad[0] / total
        minus_sign = signs[...]
        others = pairs[1 - a].reshape(1024, 1024)
        summed = lax.dot_general(units[a], others, NT, preferred_element_type=F32)
        logit = SCALE * summed + BIAS
        weights = (factor * minus_sign * jax.nn.sigmoid(minus_sign * logit)).astype(LOW)
        dot = jnp.sum(weights.astype(F32) * summed, axis=1, keepdims=True)
        d = jnp.dot(weights, others, preferred_element_type=F32)
        for t in range(8):
            piece = d[:, t * 128:(t + 1) * 128]
            d_own[a, t // NY, t % NY] = piece
            d_send[a, t // NY, t % NY] = piece.astype(LOW)
        dots[a, 0] = jnp.transpose(jnp.broadcast_to(dot, (128, 128)))[:8]
        for k in (2, 1, 3):
            send(d_send.at[a, 1 - half, y_right(k)], d_recv.at[a, 0, k], sent, got, k, y_peer(k))
            send(dots.at[a, 0], dots.at[a, k], sent, got, 4 + k, y_peer(k))
        for k in (2, 1, 3):
            send(d_send.at[a, half, y_right(k)], d_recv.at[a, 1, k], sent, got, 8 + k, y_peer(k))
        yield
        away = d_own[a, 1 - half, y]
        for k in range(1, 4):
            arrived(d_recv.at[a, 0, k], sent, got, k, y_peer(k))
            away = away + d_recv[a, 0, k].astype(F32)
        d_last[a, 0] = away.astype(LOW)
        send(d_last.at[a, 0], d_last.at[a, 1], sent, got, 0, half_peer)
        for k in range(1, 4):
            arrived(dots.at[a, k], sent, got, 4 + k, y_peer(k))
        dots[a, 4] = dots[a, 0] + dots[a, 1] + dots[a, 2] + dots[a, 3]
        send(dots.at[a, 4], dots.at[a, 5], sent, got, 4, half_peer)
        yield
        d = d_own[a, half, y]
        for k in range(1, 4):
            arrived(d_recv.at[a, 1, k], sent, got, 8 + k, y_peer(k))
            d = d + d_recv[a, 1, k].astype(F32)
        arrived(d_last.at[a, 1], sent, got, 0, half_peer)
        arrived(dots.at[a, 5], sent, got, 4, half_peer)
        d = d + d_last[a, 1].astype(F32)
        dot = jnp.transpose(jnp.broadcast_to((dots[a, 4] + dots[a, 5])[:1], (128, 128)))
        scale = inverse[a]
        grad = ((d - proj_own[a] * scale * dot) * scale).astype(LOW)

        sent, got = grad_sent.at[a], grad_got.at[a]
        for k in (2, 1, 3, 0):
            for zz in range(8):
                columns = pl.ds(pl.multiple_of((zz * NX + x_right(k)) * 128, 128), 128)
                part = lax.dot_general(features[a, :, columns], grad, TN, preferred_element_type=F32)
                part = part.reshape(2, 64, 128)
                first, second = part[0], part[1]
                own_part[a, k, zz // 4, zz % 4] = jnp.where(c == 0, first, second)
                core_send[a, k, zz // 4, zz % 4] = jnp.where(c == 0, second, first).astype(LOW)
            send(core_send.at[a, k], core_recv.at[a, k], sent, got, k, core_peer)
        yield
        for f in (1, 0):
            to = high(f)
            for k in (2, 1, 3):
                if f:
                    arrived(core_recv.at[a, k], sent, got, k, core_peer)
                x_send[a, k, to] = (own_part[a, k, to] + core_recv[a, k, to].astype(F32)).astype(LOW)
                n = 4 * (2 - f) + k
                send(x_send.at[a, k, to], x_recv.at[a, k, to], sent, got, n, x_peer(k))
        arrived(core_recv.at[a, 0], sent, got, 0, core_peer)
        z_own[a] = own_part[a, 0] + core_recv[a, 0].astype(F32)
        yield
        for f in (1, 0):
            to = high(f)
            summed = z_own[a, to]
            for k in (1, 3, 2):
                arrived(x_recv.at[a, k, to], sent, got, 4 * (2 - f) + k, x_peer(k))
                summed = summed + x_recv[a, k, to].astype(F32)
            z_own[a, to] = summed
            z_send[a, to] = summed.astype(LOW)
            for k in ((7, 6, 5, 4) if f else (3, 2, 1)):
                there = z_send.at[a, to, low(k % 4)]
                send(there, z_recv.at[a, k], sent, got, 12 + k, z_peer(k))
            if f:
                yield
        yield
        done = z_own[a, high(0), low(0)]
        for k in range(1, 8):
            arrived(z_recv.at[a, k], sent, got, 12 + k, z_peer(k))
            done = done + z_recv[a, k].astype(F32)
        (visit_out, note_out)[a][...] = done
        yield

    def mark_signs():
        own = jnp.transpose(jnp.broadcast_to(ids[pl.ds(dp, 1), :], (128, 128)))
        moved[...] = pltpu.roll(ids[...], lax.rem(128 - tensor * 16, 128), 1)
        lane = lax.div(lax.broadcasted_iota(jnp.int32, (8, 128), 1), 16)
        packed = jnp.zeros((8, 128), jnp.int32)
        for k in range(8):
            part = moved[pl.ds(k, 8, stride=8), :]
            packed = jnp.where(lane == k, pltpu.roll(part, 16 * k, 1) if k else part, packed)
        for n in range(8):
            row = packed[n:n + 1]
            signs[:, n * 128:(n + 1) * 128] = jnp.where(own == row, -1.0, 1.0).astype(F32)

    def chain(a):
        for n, _ in enumerate(gather(heads.at[a], head_sent.at[a], head_got.at[a])):
            if a == 0 and n == 2:
                for k in range(1, 4):
                    pl.semaphore_signal(
                        known, inc=1, device_id=y_peer(k), device_id_type=pl.DeviceIdType.MESH
                    )
            yield
        loads[2 + a].wait()
        yield from project(a)
        yield from gather(pairs.at[a], pair_sent.at[a], pair_got.at[a])
        yield

    loads = [
        pltpu.make_async_copy(src, dst, load_done.at[n])
        for n, (src, dst) in enumerate((
            (visit_weight, heads.at[0, high(0), low(0), x, c]),
            (note_weight, heads.at[1, high(0), low(0), x, c]),
            (visits_in, features.at[0]),
            (notes_in, features.at[1]),
            (ids_in, ids),
        ))
    ]
    for n in (4, 0, 1, 2, 3):
        loads[n].start()
    loads[4].wait()
    mark_signs()
    loads[0].wait()
    loads[1].wait()
    pl.semaphore_wait(barrier, len(peers))

    steps = {
        "a": chain(0), "b": chain(1), "c": spread(0), "d": spread(1), "A": embed(0), "B": embed(1),
    }
    for step in "".join(ORDER):
        next(steps[step])
    for copy in started:
        copy.wait_send()


def local(visits, notes, visit_weight, note_weight, patient_ids, loss_grad):
    rows = visits.shape[0]
    total = patient_ids.shape[0]
    vmem = pl.BlockSpec(memory_space=pltpu.VMEM)
    hbm = pl.BlockSpec(memory_space=pltpu.HBM)
    grad = jax.ShapeDtypeStruct(visit_weight.shape, F32)
    sems = pltpu.SemaphoreType.DMA
    return pl.pallas_call(
        functools.partial(kernel, total),
        out_shape=(grad, grad),
        in_specs=[hbm] * 5 + [pl.BlockSpec(memory_space=pltpu.SMEM)],
        out_specs=(vmem, vmem),
        scratch_shapes=[
            pltpu.VMEM((total // rows, rows), jnp.int32),
            pltpu.VMEM((total // rows, rows), jnp.int32),
            pltpu.VMEM((128, 1024), F32),
            pltpu.VMEM((2,) + visits.shape, LOW),
            pltpu.VMEM((2, 2, 4, 4, 2, 64, 128), LOW),
            pltpu.VMEM((2, 2, 4, 128, 128), LOW),
            pltpu.VMEM((2, 2, 4, 16, 128), LOW),
            pltpu.VMEM((2, 128, 128), F32),
            pltpu.VMEM((2, 128, 128), F32),
            pltpu.VMEM((2, 128, 1024), LOW),
            pltpu.VMEM((2, 2, 4, 4, 2, 16, 1024), LOW),
            pltpu.VMEM((2, 2, 4, 128, 128), F32),
            pltpu.VMEM((2, 2, 4, 128, 128), LOW),
            pltpu.VMEM((2, 2, 4, 128, 128), LOW),
            pltpu.VMEM((2, 2, 128, 128), LOW),
            pltpu.VMEM((2, 6, 8, 128), F32),
            pltpu.VMEM((2, 4, 2, 4, 64, 128), F32),
            pltpu.VMEM((2, 4, 2, 4, 64, 128), LOW),
            pltpu.VMEM((2, 4, 2, 4, 64, 128), LOW),
            pltpu.VMEM((2, 4, 2, 4, 64, 128), LOW),
            pltpu.VMEM((2, 4, 2, 4, 64, 128), LOW),
            pltpu.VMEM((2, 2, 4, 64, 128), F32),
            pltpu.VMEM((2, 2, 4, 64, 128), LOW),
            pltpu.VMEM((2, 8, 64, 128), LOW),
            sems((5,)),
            sems((2, 48)), sems((2, 48)),
            sems((2, 16)), sems((2, 16)),
            sems((2, 48)), sems((2, 48)),
            sems((2, 12)), sems((2, 12)),
            sems((2, 20)), sems((2, 20)),
            pltpu.SemaphoreType.REGULAR,
        ],
        compiler_params=pltpu.CompilerParams(
            collective_id=0, has_side_effects=True, vmem_limit_bytes=60 * 1024 * 1024
        ),
    )(visits, notes, visit_weight, note_weight, patient_ids.reshape(-1, rows), loss_grad)


def solution(mesh):
    return jax.shard_map(
        local,
        mesh=mesh,
        in_specs=(P("dp", None), P("dp", None), P("dp", "tensor"), P("dp", "tensor"), P(), P()),
        out_specs=(P("dp", "tensor"), P("dp", "tensor")),
        check_vma=False,
    )
```

```python
import functools

import jax
import jax.numpy as jnp
from jax import lax
from jax.experimental import pallas as pl
from jax.experimental.pallas import tpu as pltpu
from jax.sharding import PartitionSpec as P

SCALE = 10.0
BIAS = -2.0
EPS = 1e-06
F32 = jnp.float32
LOW = jnp.bfloat16
NT = (((1,), (1,)), ((), ()))
TN = (((0,), (0,)), ((), ()))
NX, NY = 4, 4
ORDER = (
    "aabababababababb",
    "cdab",
    "aabcdabababdab",
    "aBbBbc",
    "AABBAABBABAABA",
)


def flip(value, bit):
    return 1 - value if bit else value


def kernel(
    total,
    visits_in, notes_in, visit_weight, note_weight, ids_in, loss_grad,
    visit_out, note_out,
    ids, moved, signs, features, heads, projs, firsts, proj_own, inverse, units, pairs,
    d_own, d_send, d_recv, d_last, dots,
    own_part, core_send, core_recv, x_send, x_recv, z_own, z_send, z_recv, z_last,
    load_done, head_sent, head_got, proj_sent, proj_got, pair_sent, pair_got,
    d_sent, d_got, grad_sent, grad_got, known,
):
    dp, tensor = lax.axis_index("dp"), lax.axis_index("tensor")
    c, x, z = lax.rem(dp, 2), lax.rem(lax.div(dp, 2), NX), lax.div(dp, 2 * NX)
    z0, z1, z2 = lax.rem(z, 2), lax.rem(lax.div(z, 2), 2), lax.div(z, 4)
    y, half = lax.rem(tensor, NY), lax.div(tensor, NY)
    left, right = lax.rem(x + NX - 1, NX), lax.rem(x + 1, NX)
    beyond = lax.rem(x + 2, NX)

    def low(j):
        return flip(z1, j // 2) * 2 + flip(z0, j % 2)

    def high(f):
        return flip(z2, f)

    def at(zz, xx, cc):
        return ((zz * NX + xx) * 2 + cc, tensor)

    def z_peer(k):
        return at(high(k // 4) * 4 + low(k % 4), x, c)

    def x_right(k):
        return lax.rem(x + k, NX)

    def x_peer(k):
        return at(z, x_right(k), c)

    def y_right(k):
        return lax.rem(y + k, NY)

    def y_left(k):
        return lax.rem(y + NY - k, NY)

    def y_peer(k):
        return (dp, half * NY + y_right(k))

    core_peer = at(z, x, 1 - c)
    half_peer = (dp, (1 - half) * NY + y)
    middle_peer = (((1 - z2) * 4 + low(0)) * NX * 2 + x * 2 + c, (1 - half) * NY + y)

    started = []

    def send(src, dst, sent, got, n, peer):
        copy = pltpu.make_async_remote_copy(
            src_ref=src, dst_ref=dst, send_sem=sent.at[n], recv_sem=got.at[n],
            device_id=peer, device_id_type=pl.DeviceIdType.MESH,
        )
        copy.start()
        started.append(copy)

    def arrived(dst, sent, got, n, peer):
        pltpu.make_async_remote_copy(
            src_ref=dst, dst_ref=dst, send_sem=sent.at[n], recv_sem=got.at[n],
            device_id=peer, device_id_type=pl.DeviceIdType.MESH,
        ).wait_recv()

    peers = (
        [z_peer(k) for k in range(1, 5)] + [x_peer(k) for k in range(1, 4)]
        + [y_peer(k) for k in range(1, 4)] + [core_peer, middle_peer]
    )
    barrier = pltpu.get_barrier_semaphore()
    for peer in peers:
        pl.semaphore_signal(barrier, inc=1, device_id=peer, device_id_type=pl.DeviceIdType.MESH)

    def gather(buf, sent, got):
        def block(j, f, xx):
            return buf.at[high(f), low(j), xx, c]

        def to_z(j, f, peer, n):
            here = block(j, f, x)
            send(here, here, sent, got, 4 * f + n, z_peer(peer))

        def from_z(j, f, peer):
            arrived(block(j, f, x), sent, got, 4 * f + j, z_peer(peer))

        def to_x(j, f):
            here = block(j, f, x)
            send(here, here, sent, got, 8 + 2 * j + f, x_peer(1))
            send(here, here, sent, got, 16 + 2 * j + f, x_peer(3))

        def to_core(j, n, xx):
            chunk = buf.at[:, low(j), xx, c]
            send(chunk, chunk, sent, got, 32 + 4 * n + j, core_peer)

        mine = block(0, 0, x)
        send(mine, mine, sent, got, 0, z_peer(4))
        for j in (3, 2, 1):
            to_z(0, 0, j, j)
        to_x(0, 0)
        yield
        for j in (1, 2, 3):
            from_z(j, 0, j)
            to_x(j, 0)
        yield
        arrived(block(0, 1, x), sent, got, 0, z_peer(4))
        for j in (3, 2, 1):
            to_z(0, 1, j, j)
        to_x(0, 1)
        to_core(0, 0, x)
        yield
        for j in range(4):
            theirs = block(j, 0, left)
            arrived(theirs, sent, got, 8 + 2 * j, x_peer(3))
            send(theirs, theirs, sent, got, 24 + 2 * j, x_peer(1))
            arrived(block(j, 0, right), sent, got, 16 + 2 * j, x_peer(1))
        yield
        for j in (2, 1, 3):
            from_z(j, 1, j)
            to_x(j, 1)
            to_core(j, 0, x)
        yield
        for j in (0, 2, 1, 3):
            theirs = block(j, 1, right)
            arrived(theirs, sent, got, 17 + 2 * j, x_peer(1))
            send(theirs, theirs, sent, got, 25 + 2 * j, x_peer(3))
            arrived(block(j, 1, left), sent, got, 9 + 2 * j, x_peer(3))
            to_core(j, 1, left)
            to_core(j, 2, right)
        yield
        for j in (0, 2, 1, 3):
            arrived(block(j, 0, beyond), sent, got, 24 + 2 * j, x_peer(3))
            arrived(block(j, 1, beyond), sent, got, 25 + 2 * j, x_peer(1))
            to_core(j, 3, beyond)
        yield
        for n, xx in enumerate((x, left, right, beyond)):
            for j in range(4):
                arrived(buf.at[:, low(j), xx, 1 - c], sent, got, 32 + 4 * n + j, core_peer)

    def project(a):
        sent, got = proj_sent.at[a], proj_got.at[a]
        head = heads[a].reshape(features.shape[2], 128)
        proj = jnp.dot(features[a], head, preferred_element_type=F32)
        proj_own[a] = proj
        projs[a, half, y] = proj.astype(LOW)
        if a == 0:
            pl.semaphore_wait(known, 3)
        for f in (1, 0):
            for k in (2, 1, 3, 0):
                peer = flip(half, f) * NY + y_right(k)
                part = projs.at[a, half, y, pl.ds(pl.multiple_of(peer * 16, 16), 16)]
                if f or k:
                    send(part, firsts.at[a, half, y], sent, got, 8 + 4 * f + k, (dp, peer))
        firsts[a, half, y] = projs[a, half, y, pl.ds(pl.multiple_of(tensor * 16, 16), 16), :]
        yield
        for f in (0, 1):
            for k in range(4):
                if f or k:
                    peer = flip(half, f) * NY + y_right(k)
                    slot = firsts.at[a, flip(half, f), y_left(k)]
                    arrived(slot, sent, got, 8 + 4 * f + k, (dp, peer))
        _, rounded = normalised([firsts[a, t // NY, t % NY] for t in range(8)])
        for t in range(8):
            pairs[a, high(0), low(0), x, c, :, t * 128:(t + 1) * 128] = rounded[t]

    def spread(a):
        sent, got = proj_sent.at[a], proj_got.at[a]
        mine, other = projs.at[a, half, y], projs.at[a, 1 - half, y]
        send(mine, mine, sent, got, 0, half_peer)
        for k in (2, 1, 3):
            send(mine, mine, sent, got, k, y_peer(k))
        yield
        arrived(other, sent, got, 0, half_peer)
        for k in (2, 1, 3):
            send(other, other, sent, got, 4 + k, y_peer(k))
        yield
        for k in range(1, 4):
            arrived(projs.at[a, half, y_left(k)], sent, got, k, y_peer(k))
        for k in range(1, 4):
            arrived(projs.at[a, 1 - half, y_left(k)], sent, got, 4 + k, y_peer(k))
        scale, rounded = normalised([projs[a, t // NY, t % NY] for t in range(8)])
        inverse[a] = jnp.broadcast_to(scale, (128, 128))
        for t in range(8):
            units[a, :, t * 128:(t + 1) * 128] = rounded[t]
        yield

    def normalised(parts):
        parts = [part.astype(F32) for part in parts]
        squares = parts[0] * parts[0]
        for part in parts[1:]:
            squares = squares + part * part
        scale = lax.rsqrt(jnp.sum(squares, axis=1, keepdims=True) + EPS)
        return scale, [(part * scale).astype(LOW) for part in parts]

    def embed(a):
        sent, got = d_sent.at[a], d_got.at[a]
        factor = SCALE * loss_grad[0] / total
        minus_sign = signs[...]
        others = pairs[1 - a].reshape(1024, 1024)
        summed = lax.dot_general(units[a], others, NT, preferred_element_type=F32)
        logit = SCALE * summed + BIAS
        weights = (factor * minus_sign * jax.nn.sigmoid(minus_sign * logit)).astype(LOW)
        dot = jnp.sum(weights.astype(F32) * summed, axis=1, keepdims=True)
        d = jnp.dot(weights, others, preferred_element_type=F32)
        for t in range(8):
            piece = d[:, t * 128:(t + 1) * 128]
            d_own[a, t // NY, t % NY] = piece
            d_send[a, t // NY, t % NY] = piece.astype(LOW)
        dots[a, 0] = jnp.transpose(jnp.broadcast_to(dot, (128, 128)))[:8]
        for k in (2, 1, 3):
            send(d_send.at[a, 1 - half, y_right(k)], d_recv.at[a, 0, k], sent, got, k, y_peer(k))
            send(dots.at[a, 0], dots.at[a, k], sent, got, 4 + k, y_peer(k))
        for k in (2, 1, 3):
            send(d_send.at[a, half, y_right(k)], d_recv.at[a, 1, k], sent, got, 8 + k, y_peer(k))
        yield
        away = d_own[a, 1 - half, y]
        for k in range(1, 4):
            arrived(d_recv.at[a, 0, k], sent, got, k, y_peer(k))
            away = away + d_recv[a, 0, k].astype(F32)
        d_last[a, 0] = away.astype(LOW)
        send(d_last.at[a, 0], d_last.at[a, 1], sent, got, 0, half_peer)
        for k in range(1, 4):
            arrived(dots.at[a, k], sent, got, 4 + k, y_peer(k))
        dots[a, 4] = dots[a, 0] + dots[a, 1] + dots[a, 2] + dots[a, 3]
        send(dots.at[a, 4], dots.at[a, 5], sent, got, 4, half_peer)
        yield
        d = d_own[a, half, y]
        for k in range(1, 4):
            arrived(d_recv.at[a, 1, k], sent, got, 8 + k, y_peer(k))
            d = d + d_recv[a, 1, k].astype(F32)
        arrived(d_last.at[a, 1], sent, got, 0, half_peer)
        arrived(dots.at[a, 5], sent, got, 4, half_peer)
        d = d + d_last[a, 1].astype(F32)
        dot = jnp.transpose(jnp.broadcast_to((dots[a, 4] + dots[a, 5])[:1], (128, 128)))
        scale = inverse[a]
        grad = ((d - proj_own[a] * scale * dot) * scale).astype(LOW)

        sent, got = grad_sent.at[a], grad_got.at[a]
        for k in (2, 1, 3, 0):
            for zz in range(8):
                columns = pl.ds(pl.multiple_of((zz * NX + x_right(k)) * 128, 128), 128)
                part = lax.dot_general(features[a, :, columns], grad, TN, preferred_element_type=F32)
                part = part.reshape(2, 64, 128)
                first, second = part[0], part[1]
                own_part[a, k, zz // 4, zz % 4] = jnp.where(c == 0, first, second)
                core_send[a, k, zz // 4, zz % 4] = jnp.where(c == 0, second, first).astype(LOW)
            send(core_send.at[a, k], core_recv.at[a, k], sent, got, k, core_peer)
        yield
        for f in (1, 0):
            to = high(f)
            for k in (2, 1, 3):
                if f:
                    arrived(core_recv.at[a, k], sent, got, k, core_peer)
                x_send[a, k, to] = (own_part[a, k, to] + core_recv[a, k, to].astype(F32)).astype(LOW)
                n = 4 * (2 - f) + k
                send(x_send.at[a, k, to], x_recv.at[a, k, to], sent, got, n, x_peer(k))
        arrived(core_recv.at[a, 0], sent, got, 0, core_peer)
        z_own[a] = own_part[a, 0] + core_recv[a, 0].astype(F32)
        yield
        for f in (1, 0):
            to = high(f)
            summed = z_own[a, to]
            for k in (1, 3, 2):
                arrived(x_recv.at[a, k, to], sent, got, 4 * (2 - f) + k, x_peer(k))
                summed = summed + x_recv[a, k, to].astype(F32)
            z_own[a, to] = summed
            z_send[a, to] = summed.astype(LOW)
            for j in (3, 2, 1):
                there = z_send.at[a, to, low(j)]
                send(there, z_recv.at[a, j, to], sent, got, 4 * (4 - f) + j, z_peer(j))
            yield
        for f in (1, 0):
            done = z_own[a, high(f), low(0)]
            for j in (1, 2, 3):
                arrived(z_recv.at[a, j, high(f)], sent, got, 4 * (4 - f) + j, z_peer(j))
                done = done + z_recv[a, j, high(f)].astype(F32)
            if f:
                z_last[a, 0] = done.astype(LOW)
                send(z_last.at[a, 0], z_last.at[a, 1], sent, got, 12, z_peer(4))
                yield
        arrived(z_last.at[a, 1], sent, got, 12, z_peer(4))
        (visit_out, note_out)[a][...] = done + z_last[a, 1].astype(F32)
        yield

    def mark_signs():
        own = jnp.transpose(jnp.broadcast_to(ids[pl.ds(dp, 1), :], (128, 128)))
        moved[...] = pltpu.roll(ids[...], lax.rem(128 - tensor * 16, 128), 1)
        lane = lax.div(lax.broadcasted_iota(jnp.int32, (8, 128), 1), 16)
        packed = jnp.zeros((8, 128), jnp.int32)
        for k in range(8):
            part = moved[pl.ds(k, 8, stride=8), :]
            packed = jnp.where(lane == k, pltpu.roll(part, 16 * k, 1) if k else part, packed)
        for n in range(8):
            row = packed[n:n + 1]
            signs[:, n * 128:(n + 1) * 128] = jnp.where(own == row, -1.0, 1.0).astype(F32)

    def chain(a):
        for n, _ in enumerate(gather(heads.at[a], head_sent.at[a], head_got.at[a])):
            if a == 0 and n == 2:
                for k in range(1, 4):
                    pl.semaphore_signal(
                        known, inc=1, device_id=y_peer(k), device_id_type=pl.DeviceIdType.MESH
                    )
            yield
        loads[2 + a].wait()
        yield from project(a)
        yield from gather(pairs.at[a], pair_sent.at[a], pair_got.at[a])
        yield

    loads = [
        pltpu.make_async_copy(src, dst, load_done.at[n])
        for n, (src, dst) in enumerate((
            (visit_weight, heads.at[0, high(0), low(0), x, c]),
            (note_weight, heads.at[1, high(0), low(0), x, c]),
            (visits_in, features.at[0]),
            (notes_in, features.at[1]),
            (ids_in, ids),
        ))
    ]
    for n in (4, 0, 1, 2, 3):
        loads[n].start()
    loads[4].wait()
    mark_signs()
    loads[0].wait()
    loads[1].wait()
    pl.semaphore_wait(barrier, len(peers))

    steps = {
        "a": chain(0), "b": chain(1), "c": spread(0), "d": spread(1), "A": embed(0), "B": embed(1),
    }
    for step in "".join(ORDER):
        next(steps[step])
    for copy in started:
        copy.wait_send()


def local(visits, notes, visit_weight, note_weight, patient_ids, loss_grad):
    rows = visits.shape[0]
    total = patient_ids.shape[0]
    vmem = pl.BlockSpec(memory_space=pltpu.VMEM)
    hbm = pl.BlockSpec(memory_space=pltpu.HBM)
    grad = jax.ShapeDtypeStruct(visit_weight.shape, F32)
    sems = pltpu.SemaphoreType.DMA
    return pl.pallas_call(
        functools.partial(kernel, total),
        out_shape=(grad, grad),
        in_specs=[hbm] * 5 + [pl.BlockSpec(memory_space=pltpu.SMEM)],
        out_specs=(vmem, vmem),
        scratch_shapes=[
            pltpu.VMEM((total // rows, rows), jnp.int32),
            pltpu.VMEM((total // rows, rows), jnp.int32),
            pltpu.VMEM((128, 1024), F32),
            pltpu.VMEM((2,) + visits.shape, LOW),
            pltpu.VMEM((2, 2, 4, 4, 2, 64, 128), LOW),
            pltpu.VMEM((2, 2, 4, 128, 128), LOW),
            pltpu.VMEM((2, 2, 4, 16, 128), LOW),
            pltpu.VMEM((2, 128, 128), F32),
            pltpu.VMEM((2, 128, 128), F32),
            pltpu.VMEM((2, 128, 1024), LOW),
            pltpu.VMEM((2, 2, 4, 4, 2, 16, 1024), LOW),
            pltpu.VMEM((2, 2, 4, 128, 128), F32),
            pltpu.VMEM((2, 2, 4, 128, 128), LOW),
            pltpu.VMEM((2, 2, 4, 128, 128), LOW),
            pltpu.VMEM((2, 2, 128, 128), LOW),
            pltpu.VMEM((2, 6, 8, 128), F32),
            pltpu.VMEM((2, 4, 2, 4, 64, 128), F32),
            pltpu.VMEM((2, 4, 2, 4, 64, 128), LOW),
            pltpu.VMEM((2, 4, 2, 4, 64, 128), LOW),
            pltpu.VMEM((2, 4, 2, 4, 64, 128), LOW),
            pltpu.VMEM((2, 4, 2, 4, 64, 128), LOW),
            pltpu.VMEM((2, 2, 4, 64, 128), F32),
            pltpu.VMEM((2, 2, 4, 64, 128), LOW),
            pltpu.VMEM((2, 4, 2, 64, 128), LOW),
            pltpu.VMEM((2, 2, 64, 128), LOW),
            sems((5,)),
            sems((2, 48)), sems((2, 48)),
            sems((2, 16)), sems((2, 16)),
            sems((2, 48)), sems((2, 48)),
            sems((2, 12)), sems((2, 12)),
            sems((2, 20)), sems((2, 20)),
            pltpu.SemaphoreType.REGULAR,
        ],
        compiler_params=pltpu.CompilerParams(
            collective_id=0, has_side_effects=True, vmem_limit_bytes=60 * 1024 * 1024
        ),
    )(visits, notes, visit_weight, note_weight, patient_ids.reshape(-1, rows), loss_grad)


def solution(mesh):
    return jax.shard_map(
        local,
        mesh=mesh,
        in_specs=(P("dp", None), P("dp", None), P("dp", "tensor"), P("dp", "tensor"), P(), P()),
        out_specs=(P("dp", "tensor"), P("dp", "tensor")),
        check_vma=False,
    )
```

```python
import functools

import jax
import jax.numpy as jnp
from jax import lax
from jax.experimental import pallas as pl
from jax.experimental.pallas import tpu as pltpu
from jax.sharding import PartitionSpec as P

SCALE = 10.0
BIAS = -2.0
EPS = 1e-06
F32 = jnp.float32
LOW = jnp.bfloat16
NT = (((1,), (1,)), ((), ()))
TN = (((0,), (0,)), ((), ()))
NX, NY = 4, 4
ORDER = (
    "aabababababababb",
    "cdab",
    "aabcdabababdab",
    "aBbcBb",
    "AABBAABBABAABA",
)


def flip(value, bit):
    return 1 - value if bit else value


def kernel(
    total,
    visits_in, notes_in, visit_weight, note_weight, ids_in, loss_grad,
    visit_out, note_out,
    ids, moved, signs, features, heads, projs, firsts, proj_own, inverse, units, pairs,
    d_own, d_send, d_recv, d_last, dots,
    own_part, core_send, core_recv, x_send, x_recv, z_own, z_send, z_recv, z_last,
    load_done, head_sent, head_got, proj_sent, proj_got, pair_sent, pair_got,
    d_sent, d_got, grad_sent, grad_got, known,
):
    dp, tensor = lax.axis_index("dp"), lax.axis_index("tensor")
    c, x, z = lax.rem(dp, 2), lax.rem(lax.div(dp, 2), NX), lax.div(dp, 2 * NX)
    z0, z1, z2 = lax.rem(z, 2), lax.rem(lax.div(z, 2), 2), lax.div(z, 4)
    y, half = lax.rem(tensor, NY), lax.div(tensor, NY)
    left, right = lax.rem(x + NX - 1, NX), lax.rem(x + 1, NX)
    beyond = lax.rem(x + 2, NX)

    def low(j):
        return flip(z1, j // 2) * 2 + flip(z0, j % 2)

    def high(f):
        return flip(z2, f)

    def at(zz, xx, cc):
        return ((zz * NX + xx) * 2 + cc, tensor)

    def z_peer(k):
        return at(high(k // 4) * 4 + low(k % 4), x, c)

    def x_right(k):
        return lax.rem(x + k, NX)

    def x_peer(k):
        return at(z, x_right(k), c)

    def y_right(k):
        return lax.rem(y + k, NY)

    def y_left(k):
        return lax.rem(y + NY - k, NY)

    def y_peer(k):
        return (dp, half * NY + y_right(k))

    core_peer = at(z, x, 1 - c)
    half_peer = (dp, (1 - half) * NY + y)
    middle_peer = (((1 - z2) * 4 + low(0)) * NX * 2 + x * 2 + c, (1 - half) * NY + y)

    started = []

    def send(src, dst, sent, got, n, peer):
        copy = pltpu.make_async_remote_copy(
            src_ref=src, dst_ref=dst, send_sem=sent.at[n], recv_sem=got.at[n],
            device_id=peer, device_id_type=pl.DeviceIdType.MESH,
        )
        copy.start()
        started.append(copy)

    def arrived(dst, sent, got, n, peer):
        pltpu.make_async_remote_copy(
            src_ref=dst, dst_ref=dst, send_sem=sent.at[n], recv_sem=got.at[n],
            device_id=peer, device_id_type=pl.DeviceIdType.MESH,
        ).wait_recv()

    peers = (
        [z_peer(k) for k in range(1, 5)] + [x_peer(k) for k in range(1, 4)]
        + [y_peer(k) for k in range(1, 4)] + [core_peer, middle_peer]
    )
    barrier = pltpu.get_barrier_semaphore()
    for peer in peers:
        pl.semaphore_signal(barrier, inc=1, device_id=peer, device_id_type=pl.DeviceIdType.MESH)

    def gather(buf, sent, got):
        def block(j, f, xx):
            return buf.at[high(f), low(j), xx, c]

        def to_z(j, f, peer, n):
            here = block(j, f, x)
            send(here, here, sent, got, 4 * f + n, z_peer(peer))

        def from_z(j, f, peer):
            arrived(block(j, f, x), sent, got, 4 * f + j, z_peer(peer))

        def to_x(j, f):
            here = block(j, f, x)
            send(here, here, sent, got, 8 + 2 * j + f, x_peer(1))
            send(here, here, sent, got, 16 + 2 * j + f, x_peer(3))

        def to_core(j, n, xx):
            chunk = buf.at[:, low(j), xx, c]
            send(chunk, chunk, sent, got, 32 + 4 * n + j, core_peer)

        mine = block(0, 0, x)
        send(mine, mine, sent, got, 0, z_peer(4))
        for j in (3, 2, 1):
            to_z(0, 0, j, j)
        to_x(0, 0)
        yield
        for j in (1, 2, 3):
            from_z(j, 0, j)
            to_x(j, 0)
        yield
        arrived(block(0, 1, x), sent, got, 0, z_peer(4))
        for j in (3, 2, 1):
            to_z(0, 1, j, j)
        to_x(0, 1)
        to_core(0, 0, x)
        yield
        for j in range(4):
            theirs = block(j, 0, left)
            arrived(theirs, sent, got, 8 + 2 * j, x_peer(3))
            send(theirs, theirs, sent, got, 24 + 2 * j, x_peer(1))
            arrived(block(j, 0, right), sent, got, 16 + 2 * j, x_peer(1))
        yield
        for j in (2, 1, 3):
            from_z(j, 1, j)
            to_x(j, 1)
            to_core(j, 0, x)
        yield
        for j in (0, 2, 1, 3):
            theirs = block(j, 1, right)
            arrived(theirs, sent, got, 17 + 2 * j, x_peer(1))
            send(theirs, theirs, sent, got, 25 + 2 * j, x_peer(3))
            arrived(block(j, 1, left), sent, got, 9 + 2 * j, x_peer(3))
            to_core(j, 1, left)
            to_core(j, 2, right)
        yield
        for j in (0, 2, 1, 3):
            arrived(block(j, 0, beyond), sent, got, 24 + 2 * j, x_peer(3))
            arrived(block(j, 1, beyond), sent, got, 25 + 2 * j, x_peer(1))
            to_core(j, 3, beyond)
        yield
        for n, xx in enumerate((x, left, right, beyond)):
            for j in range(4):
                arrived(buf.at[:, low(j), xx, 1 - c], sent, got, 32 + 4 * n + j, core_peer)

    def project(a):
        sent, got = proj_sent.at[a], proj_got.at[a]
        head = heads[a].reshape(features.shape[2], 128)
        proj = jnp.dot(features[a], head, preferred_element_type=F32)
        proj_own[a] = proj
        projs[a, half, y] = proj.astype(LOW)
        if a == 0:
            pl.semaphore_wait(known, 3)
        for f in (1, 0):
            for k in (2, 1, 3, 0):
                peer = flip(half, f) * NY + y_right(k)
                part = projs.at[a, half, y, pl.ds(pl.multiple_of(peer * 16, 16), 16)]
                if f or k:
                    send(part, firsts.at[a, half, y], sent, got, 8 + 4 * f + k, (dp, peer))
        firsts[a, half, y] = projs[a, half, y, pl.ds(pl.multiple_of(tensor * 16, 16), 16), :]
        yield
        for f in (0, 1):
            for k in range(4):
                if f or k:
                    peer = flip(half, f) * NY + y_right(k)
                    slot = firsts.at[a, flip(half, f), y_left(k)]
                    arrived(slot, sent, got, 8 + 4 * f + k, (dp, peer))
        _, rounded = normalised([firsts[a, t // NY, t % NY] for t in range(8)])
        for t in range(8):
            pairs[a, high(0), low(0), x, c, :, t * 128:(t + 1) * 128] = rounded[t]

    def spread(a):
        sent, got = proj_sent.at[a], proj_got.at[a]
        mine, other = projs.at[a, half, y], projs.at[a, 1 - half, y]
        send(mine, mine, sent, got, 0, half_peer)
        for k in (2, 1, 3):
            send(mine, mine, sent, got, k, y_peer(k))
        yield
        arrived(other, sent, got, 0, half_peer)
        for k in (2, 1, 3):
            send(other, other, sent, got, 4 + k, y_peer(k))
        yield
        for k in range(1, 4):
            arrived(projs.at[a, half, y_left(k)], sent, got, k, y_peer(k))
        for k in range(1, 4):
            arrived(projs.at[a, 1 - half, y_left(k)], sent, got, 4 + k, y_peer(k))
        scale, rounded = normalised([projs[a, t // NY, t % NY] for t in range(8)])
        inverse[a] = jnp.broadcast_to(scale, (128, 128))
        for t in range(8):
            units[a, :, t * 128:(t + 1) * 128] = rounded[t]
        yield

    def normalised(parts):
        parts = [part.astype(F32) for part in parts]
        squares = parts[0] * parts[0]
        for part in parts[1:]:
            squares = squares + part * part
        scale = lax.rsqrt(jnp.sum(squares, axis=1, keepdims=True) + EPS)
        return scale, [(part * scale).astype(LOW) for part in parts]

    def embed(a):
        sent, got = d_sent.at[a], d_got.at[a]
        factor = SCALE * loss_grad[0] / total
        minus_sign = signs[...]
        others = pairs[1 - a].reshape(1024, 1024)
        summed = lax.dot_general(units[a], others, NT, preferred_element_type=F32)
        logit = SCALE * summed + BIAS
        weights = (factor * minus_sign * jax.nn.sigmoid(minus_sign * logit)).astype(LOW)
        dot = jnp.sum(weights.astype(F32) * summed, axis=1, keepdims=True)
        d = jnp.dot(weights, others, preferred_element_type=F32)
        for t in range(8):
            piece = d[:, t * 128:(t + 1) * 128]
            d_own[a, t // NY, t % NY] = piece
            d_send[a, t // NY, t % NY] = piece.astype(LOW)
        dots[a, 0] = jnp.transpose(jnp.broadcast_to(dot, (128, 128)))[:8]
        for k in (2, 1, 3):
            send(d_send.at[a, 1 - half, y_right(k)], d_recv.at[a, 0, k], sent, got, k, y_peer(k))
            send(dots.at[a, 0], dots.at[a, k], sent, got, 4 + k, y_peer(k))
        for k in (2, 1, 3):
            send(d_send.at[a, half, y_right(k)], d_recv.at[a, 1, k], sent, got, 8 + k, y_peer(k))
        yield
        away = d_own[a, 1 - half, y]
        for k in range(1, 4):
            arrived(d_recv.at[a, 0, k], sent, got, k, y_peer(k))
            away = away + d_recv[a, 0, k].astype(F32)
        d_last[a, 0] = away.astype(LOW)
        send(d_last.at[a, 0], d_last.at[a, 1], sent, got, 0, half_peer)
        for k in range(1, 4):
            arrived(dots.at[a, k], sent, got, 4 + k, y_peer(k))
        dots[a, 4] = dots[a, 0] + dots[a, 1] + dots[a, 2] + dots[a, 3]
        send(dots.at[a, 4], dots.at[a, 5], sent, got, 4, half_peer)
        yield
        d = d_own[a, half, y]
        for k in range(1, 4):
            arrived(d_recv.at[a, 1, k], sent, got, 8 + k, y_peer(k))
            d = d + d_recv[a, 1, k].astype(F32)
        arrived(d_last.at[a, 1], sent, got, 0, half_peer)
        arrived(dots.at[a, 5], sent, got, 4, half_peer)
        d = d + d_last[a, 1].astype(F32)
        dot = jnp.transpose(jnp.broadcast_to((dots[a, 4] + dots[a, 5])[:1], (128, 128)))
        scale = inverse[a]
        grad = ((d - proj_own[a] * scale * dot) * scale).astype(LOW)

        sent, got = grad_sent.at[a], grad_got.at[a]
        for k in (2, 1, 3, 0):
            for zz in range(8):
                columns = pl.ds(pl.multiple_of((zz * NX + x_right(k)) * 128, 128), 128)
                part = lax.dot_general(features[a, :, columns], grad, TN, preferred_element_type=F32)
                part = part.reshape(2, 64, 128)
                first, second = part[0], part[1]
                own_part[a, k, zz // 4, zz % 4] = jnp.where(c == 0, first, second)
                core_send[a, k, zz // 4, zz % 4] = jnp.where(c == 0, second, first).astype(LOW)
            send(core_send.at[a, k], core_recv.at[a, k], sent, got, k, core_peer)
        yield
        for f in (1, 0):
            to = high(f)
            for k in (2, 1, 3):
                if f:
                    arrived(core_recv.at[a, k], sent, got, k, core_peer)
                x_send[a, k, to] = (own_part[a, k, to] + core_recv[a, k, to].astype(F32)).astype(LOW)
                n = 4 * (2 - f) + k
                send(x_send.at[a, k, to], x_recv.at[a, k, to], sent, got, n, x_peer(k))
        arrived(core_recv.at[a, 0], sent, got, 0, core_peer)
        z_own[a] = own_part[a, 0] + core_recv[a, 0].astype(F32)
        yield
        for f in (1, 0):
            to = high(f)
            summed = z_own[a, to]
            for k in (1, 3, 2):
                arrived(x_recv.at[a, k, to], sent, got, 4 * (2 - f) + k, x_peer(k))
                summed = summed + x_recv[a, k, to].astype(F32)
            z_own[a, to] = summed
            z_send[a, to] = summed.astype(LOW)
            for j in (3, 2, 1):
                there = z_send.at[a, to, low(j)]
                send(there, z_recv.at[a, j, to], sent, got, 4 * (4 - f) + j, z_peer(j))
            yield
        for f in (1, 0):
            done = z_own[a, high(f), low(0)]
            for j in (1, 2, 3):
                arrived(z_recv.at[a, j, high(f)], sent, got, 4 * (4 - f) + j, z_peer(j))
                done = done + z_recv[a, j, high(f)].astype(F32)
            if f:
                z_last[a, 0] = done.astype(LOW)
                send(z_last.at[a, 0], z_last.at[a, 1], sent, got, 12, z_peer(4))
                yield
        arrived(z_last.at[a, 1], sent, got, 12, z_peer(4))
        (visit_out, note_out)[a][...] = done + z_last[a, 1].astype(F32)
        yield

    def mark_signs():
        own = jnp.transpose(jnp.broadcast_to(ids[pl.ds(dp, 1), :], (128, 128)))
        moved[...] = pltpu.roll(ids[...], lax.rem(128 - tensor * 16, 128), 1)
        lane = lax.div(lax.broadcasted_iota(jnp.int32, (8, 128), 1), 16)
        packed = jnp.zeros((8, 128), jnp.int32)
        for k in range(8):
            part = moved[pl.ds(k, 8, stride=8), :]
            packed = jnp.where(lane == k, pltpu.roll(part, 16 * k, 1) if k else part, packed)
        for n in range(8):
            row = packed[n:n + 1]
            signs[:, n * 128:(n + 1) * 128] = jnp.where(own == row, -1.0, 1.0).astype(F32)

    def chain(a):
        for n, _ in enumerate(gather(heads.at[a], head_sent.at[a], head_got.at[a])):
            if a == 0 and n == 2:
                for k in range(1, 4):
                    pl.semaphore_signal(
                        known, inc=1, device_id=y_peer(k), device_id_type=pl.DeviceIdType.MESH
                    )
            yield
        loads[2 + a].wait()
        yield from project(a)
        yield from gather(pairs.at[a], pair_sent.at[a], pair_got.at[a])
        yield

    loads = [
        pltpu.make_async_copy(src, dst, load_done.at[n])
        for n, (src, dst) in enumerate((
            (visit_weight, heads.at[0, high(0), low(0), x, c]),
            (note_weight, heads.at[1, high(0), low(0), x, c]),
            (visits_in, features.at[0]),
            (notes_in, features.at[1]),
            (ids_in, ids),
        ))
    ]
    for n in (4, 0, 1, 2, 3):
        loads[n].start()
    loads[4].wait()
    mark_signs()
    loads[0].wait()
    loads[1].wait()
    pl.semaphore_wait(barrier, len(peers))

    steps = {
        "a": chain(0), "b": chain(1), "c": spread(0), "d": spread(1), "A": embed(0), "B": embed(1),
    }
    for step in "".join(ORDER):
        next(steps[step])
    for copy in started:
        copy.wait_send()


def local(visits, notes, visit_weight, note_weight, patient_ids, loss_grad):
    rows = visits.shape[0]
    total = patient_ids.shape[0]
    vmem = pl.BlockSpec(memory_space=pltpu.VMEM)
    hbm = pl.BlockSpec(memory_space=pltpu.HBM)
    grad = jax.ShapeDtypeStruct(visit_weight.shape, F32)
    sems = pltpu.SemaphoreType.DMA
    return pl.pallas_call(
        functools.partial(kernel, total),
        out_shape=(grad, grad),
        in_specs=[hbm] * 5 + [pl.BlockSpec(memory_space=pltpu.SMEM)],
        out_specs=(vmem, vmem),
        scratch_shapes=[
            pltpu.VMEM((total // rows, rows), jnp.int32),
            pltpu.VMEM((total // rows, rows), jnp.int32),
            pltpu.VMEM((128, 1024), F32),
            pltpu.VMEM((2,) + visits.shape, LOW),
            pltpu.VMEM((2, 2, 4, 4, 2, 64, 128), LOW),
            pltpu.VMEM((2, 2, 4, 128, 128), LOW),
            pltpu.VMEM((2, 2, 4, 16, 128), LOW),
            pltpu.VMEM((2, 128, 128), F32),
            pltpu.VMEM((2, 128, 128), F32),
            pltpu.VMEM((2, 128, 1024), LOW),
            pltpu.VMEM((2, 2, 4, 4, 2, 16, 1024), LOW),
            pltpu.VMEM((2, 2, 4, 128, 128), F32),
            pltpu.VMEM((2, 2, 4, 128, 128), LOW),
            pltpu.VMEM((2, 2, 4, 128, 128), LOW),
            pltpu.VMEM((2, 2, 128, 128), LOW),
            pltpu.VMEM((2, 6, 8, 128), F32),
            pltpu.VMEM((2, 4, 2, 4, 64, 128), F32),
            pltpu.VMEM((2, 4, 2, 4, 64, 128), LOW),
            pltpu.VMEM((2, 4, 2, 4, 64, 128), LOW),
            pltpu.VMEM((2, 4, 2, 4, 64, 128), LOW),
            pltpu.VMEM((2, 4, 2, 4, 64, 128), LOW),
            pltpu.VMEM((2, 2, 4, 64, 128), F32),
            pltpu.VMEM((2, 2, 4, 64, 128), LOW),
            pltpu.VMEM((2, 4, 2, 64, 128), LOW),
            pltpu.VMEM((2, 2, 64, 128), LOW),
            sems((5,)),
            sems((2, 48)), sems((2, 48)),
            sems((2, 16)), sems((2, 16)),
            sems((2, 48)), sems((2, 48)),
            sems((2, 12)), sems((2, 12)),
            sems((2, 20)), sems((2, 20)),
            pltpu.SemaphoreType.REGULAR,
        ],
        compiler_params=pltpu.CompilerParams(
            collective_id=0, has_side_effects=True, vmem_limit_bytes=60 * 1024 * 1024
        ),
    )(visits, notes, visit_weight, note_weight, patient_ids.reshape(-1, rows), loss_grad)


def solution(mesh):
    return jax.shard_map(
        local,
        mesh=mesh,
        in_specs=(P("dp", None), P("dp", None), P("dp", "tensor"), P("dp", "tensor"), P(), P()),
        out_specs=(P("dp", "tensor"), P("dp", "tensor")),
        check_vma=False,
    )
```
